32 devices in a mesh: tensor: 4 (over x, core), frames: 8 (over z, y).
Axes of the slice: x: 2, y: 2, z: 4, core: 2. Of those that a mesh axis runs over, the one named last changes fastest.
Arguments:
- tokens: bfloat16 [8, 8, 256, 1024], P('frames', None, 'tensor'), may hold values from -6 to 6
- codes: int32 [8, 8], P('frames'), may hold values from 0 to 7
- table: bfloat16 [8, 1024], replicated, may hold values from -6 to 6
- gain_space: bfloat16 [1024], replicated, may hold values from 0.5 to 1.5
- gain_time: bfloat16 [1024], replicated, may hold values from 0.5 to 1.5
- gain_ffn: bfloat16 [1024], replicated, may hold values from 0.5 to 1.5
- w_qkv_space: bfloat16 [1024, 3, 1024], P(None, None, 'tensor'), may hold values from -0.1875 to 0.1875
- w_out_space: bfloat16 [1024, 1024], P('tensor'), may hold values from -1.5 to 1.5
- w_qkv_time: bfloat16 [1024, 3, 1024], P(None, None, 'tensor'), may hold values from -0.1875 to 0.1875
- w_out_time: bfloat16 [1024, 1024], P('tensor'), may hold values from -0.75 to 0.75
- w_up: bfloat16 [1024, 4096], P(None, 'tensor'), may hold values from -0.1875 to 0.1875
- w_down: bfloat16 [4096, 1024], P('tensor'), may hold values from -0.09375 to 0.09375
- cotangent: bfloat16 [8, 8, 256, 1024], P('frames', None, 'tensor'), may hold values from -6 to 6
Outputs:
- mixed: bfloat16 [8, 8, 256, 1024], P('frames', None, 'tensor')
- grad_tokens: float32 [8, 8, 256, 1024], P('frames', None, 'tensor')
- grad_table: float32 [8, 1024], replicated
- grad_gain_space: float32 [1024], replicated
- grad_gain_time: float32 [1024], replicated
- grad_gain_ffn: float32 [1024], replicated
- grad_qkv_space: float32 [1024, 3, 1024], P(None, None, 'tensor')
- grad_out_space: float32 [1024, 1024], P('tensor')
- grad_qkv_time: float32 [1024, 3, 1024], P(None, None, 'tensor')
- grad_out_time: float32 [1024, 1024], P('tensor')
- grad_up: float32 [1024, 4096], P(None, 'tensor')
- grad_down: float32 [4096, 1024], P('tensor')
The draws below stay inside these ranges and needn't reach their ends.
All inputs are finite; a program needn't handle non-finite values.
Results may differ from the reference program's by a relative error of at most 0.019.
Values may be sent and summed in bfloat16 or wider, within the bound.
A program may use at most 576 MiB of HBM per device.

```python
import jax
import jax.numpy as jnp
from jax import lax

D = 1024
H = 16
HD = 64
FF = 4096
ACTIONS = 8
S = 256
CLIPS = 8
FRAMES = 8


def place_ends(array, key, least, high):
    index_at = [jax.random.randint(jax.random.fold_in(key, axis), (), 0, length) for axis, length in enumerate(array.shape)]
    widest = array.shape.index(max(array.shape))
    neighbour = index_at[:widest] + [(index_at[widest] + 1) % array.shape[widest]] + index_at[widest + 1:]
    return array.at[tuple(index_at)].set(least).at[tuple(neighbour)].set(high)


def level_of(own_key, dims, split, least, top_value):
    level = 1.0
    for axis_at, shards_of in split:
        heights = jax.random.uniform(jax.random.fold_in(jax.random.fold_in(own_key, 6), axis_at), (shards_of,), jnp.float32, least / len(split), top_value / len(split))
        level = level * jnp.repeat(jnp.exp(heights), dims[axis_at] // shards_of).reshape((-1,) + (1,) * (len(dims) - 1 - axis_at))
    return level


def centred(rng, dims, spread, most, pieces=(), held_as=jnp.bfloat16):
    values = spread * jax.random.normal(rng, dims, jnp.float32)
    if pieces:
        values = values * level_of(rng, dims, pieces, -0.22, 0.18)
    return jnp.clip(values, -most, most).astype(held_as)


def setup_inputs(seed: int = 0) -> dict:
    key_of = jax.random.split(jax.random.key(seed), 14)
    tokens = centred(key_of[0], (FRAMES, CLIPS, S, D), 1.0, 6.0, ((0, 8), (2, 4)))
    codes = place_ends(jax.random.randint(key_of[1], (FRAMES, CLIPS), 0, ACTIONS), jax.random.fold_in(key_of[1], 1), 0, ACTIONS - 1).astype(jnp.int32)
    table = centred(key_of[2], (ACTIONS, D), 1.0, 6.0)
    gain_space = jnp.clip(1.0 + 0.1 * jax.random.normal(key_of[3], (D,), jnp.float32), 0.5, 1.5).astype(jnp.bfloat16)
    gain_time = jnp.clip(1.0 + 0.1 * jax.random.normal(key_of[4], (D,), jnp.float32), 0.5, 1.5).astype(jnp.bfloat16)
    gain_ffn = jnp.clip(1.0 + 0.1 * jax.random.normal(key_of[5], (D,), jnp.float32), 0.5, 1.5).astype(jnp.bfloat16)
    w_qkv_space = centred(key_of[6], (D, 3, H * HD), D ** -0.5, 0.1875, ((2, 4),))
    w_out_space = centred(key_of[7], (H * HD, D), (H * HD // 64) ** -0.5, 1.5, ((0, 4),))
    w_qkv_time = centred(key_of[8], (D, 3, H * HD), D ** -0.5, 0.1875, ((2, 4),))
    w_out_time = centred(key_of[9], (H * HD, D), (H * HD // 16) ** -0.5, 0.75, ((0, 4),))
    w_up = centred(key_of[10], (D, FF), D ** -0.5, 0.1875, ((1, 4),))
    w_down = centred(key_of[11], (FF, D), FF ** -0.5, 0.09375, ((0, 4),))
    cotangent = centred(key_of[12], (FRAMES, CLIPS, S, D), 1.0, 6.0, ((0, 8), (2, 4)))
    return dict(tokens=tokens, codes=codes, table=table, gain_space=gain_space, gain_time=gain_time, gain_ffn=gain_ffn, w_qkv_space=w_qkv_space, w_out_space=w_out_space, w_qkv_time=w_qkv_time, w_out_time=w_out_time, w_up=w_up, w_down=w_down, cotangent=cotangent)


EPS = 1e-06

@jax.custom_vjp
def low(v):
    return lax.optimization_barrier(v.astype(jnp.bfloat16)).astype(jnp.float32)

@jax.custom_vjp
def low_back(v):
    return v

def low_keep(v):
    return (low(v), None)

def low_pass(kept, grad):
    return (grad,)

def back_keep(v):
    return (v, None)

def back_low(kept, grad):
    return (low(grad),)
low.defvjp(low_keep, low_pass)
low_back.defvjp(back_keep, back_low)

def product(form, left, right):
    return jnp.einsum(form, left, right, precision=lax.Precision.HIGHEST)

def norm_rows(values, gain_vec):
    factor = lax.rsqrt(lax.optimization_barrier(jnp.mean(values * values, axis=-1, keepdims=True)) + EPS)
    return values * factor * gain_vec

def softmax_rows(scores):
    largest = lax.optimization_barrier(jnp.max(scores, axis=-1, keepdims=True))
    raised = jnp.exp(scores - largest)
    return raised / lax.optimization_barrier(jnp.sum(raised, axis=-1, keepdims=True))

def split_heads(packed, member):
    picked = low(low_back(packed[:, :, member, :]))
    return picked.reshape(packed.shape[0], packed.shape[1], -1, HD)

def clip_forward(stream, one_hot, table, gain_space, gain_time, gain_ffn, w_qkv_space, w_out_space, w_qkv_time, w_out_time, w_up, w_down):
    frame_count = stream.shape[0]
    positions = stream.shape[1]
    score_scale = HD ** (-0.5)
    stream_zero = stream + product('fk,kd->fd', one_hot, table)[:, None, :]
    normed = low(norm_rows(stream_zero, gain_space))
    packed = product('fsd,dke->fske', normed, w_qkv_space)
    queries = split_heads(packed, 0)
    keys_in = split_heads(packed, 1)
    values = split_heads(packed, 2)
    scores = low_back(product('fshe,fthe->fhst', queries, keys_in) * score_scale)
    soft_weights = softmax_rows(scores)
    attended = product('fhst,fthe->fshe', low(soft_weights), values)
    attended = low(low_back(attended)).reshape(frame_count, positions, -1)
    stream_one = stream_zero + low_back(product('fse,ed->fsd', attended, w_out_space))
    normed = low(norm_rows(stream_one, gain_time))
    packed = product('fsd,dke->fske', normed, w_qkv_time)
    queries = split_heads(packed, 0)
    keys_in = split_heads(packed, 1)
    values = split_heads(packed, 2)
    scores = low_back(product('fshe,gshe->shfg', queries, keys_in) * score_scale)
    frame_idx = jnp.arange(frame_count, dtype=jnp.int32)
    scores = jnp.where(frame_idx[None, :] <= frame_idx[:, None], scores, -1e+30)
    soft_weights = softmax_rows(scores)
    attended = product('shfg,gshe->fshe', low(soft_weights), values)
    attended = low(low_back(attended)).reshape(frame_count, positions, -1)
    stream_two = stream_one + low_back(product('fse,ed->fsd', attended, w_out_time))
    normed = low(norm_rows(stream_two, gain_ffn))
    hidden_pre = low_back(product('fsd,dh->fsh', normed, w_up))
    activated = low(jax.nn.gelu(hidden_pre))
    return stream_two + low_back(product('fsh,hd->fsd', activated, w_down))

def reference(tokens, codes, table, gain_space, gain_time, gain_ffn, w_qkv_space, w_out_space, w_qkv_time, w_out_time, w_up, w_down, cotangent):
    params = tuple((item.astype(jnp.float32) for item in (table, gain_space, gain_time, gain_ffn, w_qkv_space, w_out_space, w_qkv_time, w_out_time, w_up, w_down)))
    clip_inputs = (jnp.moveaxis(tokens.astype(jnp.float32), 1, 0), jnp.moveaxis(codes, 1, 0), jnp.moveaxis(cotangent.astype(jnp.float32), 1, 0))
    initial = tuple((jnp.zeros_like(item) for item in params))

    def per_clip(totals, clip_data):
        stream, clip_codes, clip_grad = clip_data
        one_hot = (clip_codes[:, None] == jnp.arange(ACTIONS, dtype=jnp.int32)[None, :]).astype(jnp.float32)

        def forward(stream_arg, *param_args):
            return clip_forward(stream_arg, one_hot, *param_args)
        result, pullback = jax.vjp(forward, stream, *params)
        gradients = pullback(clip_grad)
        totals = tuple((left + right for left, right in zip(totals, gradients[1:])))
        return (totals, (result, gradients[0]))
    totals, (results, grad_stream) = lax.scan(per_clip, initial, clip_inputs)
    mixed = jnp.moveaxis(results, 0, 1).astype(jnp.bfloat16)
    grad_tokens = jnp.moveaxis(grad_stream, 0, 1)
    return (mixed, grad_tokens, totals[0], totals[1], totals[2], totals[3], totals[4], totals[5], totals[6], totals[7], totals[8], totals[9])
```

```python
import functools

import jax
import jax.numpy as jnp
from jax import lax
from jax.experimental import pallas as pl
from jax.experimental.pallas import tpu as pltpu
from jax.sharding import PartitionSpec as P

HD = 64
EPS = 1e-06
BF = jnp.bfloat16
F32 = jnp.float32
MESH = pl.DeviceIdType.MESH
LIMIT = 63 * 1024 * 1024
LAG = 5
GAP = 2
CHUNKS = 8


def dot(left, right, contract):
    return lax.dot_general(left, right, ((contract[:1], contract[1:]), ((), ())), preferred_element_type=F32)


def norm_parts(values):
    factor = lax.rsqrt(jnp.mean(values * values, axis=-1, keepdims=True) + EPS)
    return values * factor, factor


def norm_backward(grad_normed, stream, gain_vec):
    unit, factor = norm_parts(stream)
    scaled = grad_normed * gain_vec
    grad_stream = (scaled - unit * jnp.mean(scaled * unit, axis=-1, keepdims=True)) * factor
    return grad_stream, jnp.sum(grad_normed * unit, axis=0, keepdims=True)


def head_mask(rows, width, head):
    lane = lax.broadcasted_iota(jnp.int32, (rows, width), 1)
    return (lane >= head * HD) & (lane < (head + 1) * HD)


def visible(rows, frames, query_dim=0):
    part = rows // 4
    spots = part // frames
    row = lax.broadcasted_iota(jnp.int32, (rows, rows), query_dim)
    col = lax.broadcasted_iota(jnp.int32, (rows, rows), 1 - query_dim)
    same_part = row // part == col // part
    same_spot = row % spots == col % spots
    earlier = (col % part) // spots <= (row % part) // spots
    return same_part & same_spot & earlier


def block_probs(queries, keys_in, seen):
    scores = dot(queries, keys_in, (1, 1))
    if seen is not None:
        scores = jnp.where(seen[...] > 0, scores, -1e30)
    raised = jnp.exp(scores - jnp.max(scores, axis=-1, keepdims=True))
    return raised * (1.0 / jnp.sum(raised, axis=-1, keepdims=True))


def attend(queries, keys_in, values, seen):
    rows, width = queries.shape
    total = jnp.zeros((rows, width), F32)
    queries = queries * BF(HD ** (-0.5))
    for head in range(width // HD):
        mine = head_mask(rows, width, head)
        probs = block_probs(jnp.where(mine, queries, 0), keys_in, seen)
        total = total + dot(probs.astype(BF), jnp.where(mine, values, 0), (1, 0))
    return total.astype(BF)


def attend_back(queries, keys_in, values, grad_att, seen):
    rows, width = queries.shape
    zero = jnp.zeros((rows, width), F32)
    grad_q, grad_k, grad_v = zero, zero, zero
    scale = BF(HD ** (-0.5))
    queries = queries * scale
    scaled_keys = keys_in * scale
    for head in range(width // HD):
        mine = head_mask(rows, width, head)
        my_queries = jnp.where(mine, queries, 0)
        my_grad = jnp.where(mine, grad_att, 0)
        scores = dot(keys_in, my_queries, (1, 1))
        if seen is not None:
            scores = jnp.where(seen[...] > 0, scores, -1e30)
        raised = jnp.exp(scores - jnp.max(scores, axis=0, keepdims=True))
        probs = raised * (1.0 / jnp.sum(raised, axis=0, keepdims=True))
        grad_probs = dot(values, my_grad, (1, 1))
        row_dot = jnp.sum(grad_probs * probs, axis=0, keepdims=True)
        grad_scores = (probs * (grad_probs - row_dot)).astype(BF)
        grad_q = grad_q + dot(grad_scores, jnp.where(mine, scaled_keys, 0), (0, 0))
        grad_k = grad_k + dot(grad_scores, my_queries, (1, 0))
        grad_v = grad_v + dot(probs.astype(BF), my_grad, (1, 0))
    return grad_q.astype(BF), grad_k.astype(BF), grad_v.astype(BF)


class Group:
    def __init__(self, frames=1, all_frames=False):
        me = lax.axis_index("tensor")
        self.x, self.c = me // 2, me % 2
        self.me = me
        self.chip_peer = 2 * (1 - self.x) + self.c
        self.core_peer = 2 * self.x + 1 - self.c
        self.levels = frames.bit_length() - 1
        self.bits, self.partners = [], []
        self.frames, self.all_frames = frames, all_frames
        self.frame = frame = lax.axis_index("frames")
        for level in range(self.levels):
            bit = (frame // 2**level) % 2
            self.bits.append(bit)
            self.partners.append(frame + (1 - 2 * bit) * 2**level)

    def everyone(self):
        return [("tensor", self.chip_peer), ("tensor", self.core_peer)] + [
            ("frames", partner) for partner in self.partners
        ]

    def other_frame(self, distance):
        return (self.frame + distance) % self.frames

    def meet(self):
        barrier = pltpu.get_barrier_semaphore()
        peers = self.everyone()
        if self.all_frames:
            peers = peers[:2] + [("frames", self.other_frame(far)) for far in range(1, self.frames)]
        for axis, peer in peers:
            pl.semaphore_signal(barrier, inc=1, device_id={axis: peer}, device_id_type=MESH)
        pl.semaphore_wait(barrier, len(peers))


def remote(src, dst, sems, kind, block, peer, axis="tensor"):
    return pltpu.make_async_remote_copy(
        src_ref=src,
        dst_ref=dst,
        send_sem=sems.at[0, kind, block],
        recv_sem=sems.at[1, kind, block],
        device_id={axis: peer},
        device_id_type=MESH,
    )


class Gather:
    def __init__(self, group, whole, sems):
        self.group, self.whole, self.sems = group, whole, sems

    def copy(self, kind, block):
        g = self.group
        quarter = self.whole.at[block, g.chip_peer if kind == 2 else g.me]
        return remote(quarter, quarter, self.sems, kind, block, g.chip_peer if kind == 0 else g.core_peer)

    def start(self, block):
        self.copy(0, block).start()
        self.copy(1, block).start()

    def forward(self, block):
        self.copy(0, block).wait_recv()
        self.copy(2, block).start()

    def arrive(self, block):
        self.copy(1, block).wait_recv()
        self.copy(2, block).wait_recv()

    def sent(self, block):
        for kind in range(3):
            self.copy(kind, block).wait_send()

    @staticmethod
    def scratch(blocks):
        return pltpu.SemaphoreType.DMA((2, 3, blocks))


class Scatter:
    def __init__(self, group, kept, near_out, near_in, far_out, far_in, sems):
        self.group, self.kept, self.sems = group, kept, sems
        self.near_out, self.near_in, self.far_out, self.far_in = near_out, near_in, far_out, far_in
        self.slots, self.blocks = near_out.shape[0], sems.shape[2]

    def near(self, block):
        slot = block % self.slots
        return remote(self.near_out.at[slot], self.near_in.at[slot], self.sems, 0, block, self.group.core_peer)

    def far(self, block):
        slot = block % self.slots
        return remote(self.far_out.at[slot], self.far_in.at[slot], self.sems, 1, block, self.group.chip_peer)

    def free(self, block):
        if self.blocks > self.slots:

            @pl.when(block >= self.slots)
            def _():
                self.near(block - self.slots).wait_send()
                self.far(block - self.slots).wait_send()

    def put(self, block, values, more=False):
        slot = block % self.slots
        for x in range(2):
            first, second = (values[(2 * x + c) * self.part : (2 * x + c + 1) * self.part] for c in range(2))
            own = jnp.where(self.group.c == 0, first, second)
            given = jnp.where(self.group.c == 0, second, first)
            if more:
                own = own + self.kept[slot, x]
                given = given + self.near_out[slot, x].astype(F32)
            self.kept[slot, x] = own
            self.near_out[slot, x] = given.astype(BF)

    def send(self, block, values, more=False):
        self.put(block, values, more)
        self.near(block).start()

    @property
    def part(self):
        return self.kept.shape[2]

    def cross(self, block):
        x, slot = 1 - self.group.x, block % self.slots
        self.near(block).wait_recv()
        self.far_out[slot] = (self.kept[slot, x] + self.near_in[slot, x].astype(F32)).astype(BF)
        self.far(block).start()

    def take(self, block):
        x, slot = self.group.x, block % self.slots
        self.far(block).wait_recv()
        return self.kept[slot, x] + self.near_in[slot, x].astype(F32) + self.far_in[slot].astype(F32)

    def finish(self):
        def sent(block, carry):
            self.near(block).wait_send()
            self.far(block).wait_send()
            return carry

        lax.fori_loop(self.blocks - self.slots, self.blocks, sent, 0)

    @staticmethod
    def scratch(blocks, slots, part, width):
        return [
            pltpu.VMEM((slots, 2, part, width), F32),
            pltpu.VMEM((slots, 2, part, width), BF),
            pltpu.VMEM((slots, 2, part, width), BF),
            pltpu.VMEM((slots, part, width), BF),
            pltpu.VMEM((slots, part, width), BF),
            pltpu.SemaphoreType.DMA((2, 2, blocks)),
        ]


def packed_shape(blocks, frames, part, width):
    spots = part // frames
    cuts = max(1, 16 // spots)
    return (blocks, frames, cuts * spots, width // cuts)


def pack(values, frames):
    rows, width = values.shape
    spots = rows // frames
    cuts = max(1, 16 // spots)
    wide = width // cuts
    return [
        jnp.concatenate(
            [values[frame * spots : (frame + 1) * spots, k * wide : (k + 1) * wide] for k in range(cuts)], axis=0
        )
        for frame in range(frames)
    ]


def unpack(packed, width):
    frames, rows, wide = packed.shape
    cuts = width // wide
    spots = rows // cuts
    packed = packed.astype(F32)
    return jnp.concatenate(
        [
            jnp.concatenate([packed[frame, k * spots : (k + 1) * spots] for k in range(cuts)], axis=1)
            for frame in range(frames)
        ],
        axis=0,
    )


class Exchange:
    def __init__(self, group, stage, landing, sems):
        self.group, self.stage, self.landing, self.sems = group, stage, landing, sems

    def copy(self, block, far):
        g = self.group
        other = g.other_frame(far)
        return remote(
            self.stage.at[block, other], self.landing.at[block, g.frame], self.sems, far - 1, block, other, "frames"
        )

    def push(self, block, values):
        frames = self.group.frames
        for frame, piece in enumerate(pack(values, frames)):
            self.stage[block, frame] = piece.astype(BF)
        self.landing[block, self.group.frame] = self.stage[block, self.group.frame]
        for far in range(1, frames):
            self.copy(block, far).start()

    def arrive(self, block):
        for far in range(1, self.group.frames):
            self.copy(block, far).wait_recv()

    def sent(self, block):
        for far in range(1, self.group.frames):
            self.copy(block, far).wait_send()

    @staticmethod
    def scratch(shape):
        return [pltpu.VMEM(shape, BF), pltpu.SemaphoreType.DMA((2, shape[1] - 1, shape[0]))]


class Reduce:
    def __init__(self, group_size, slack, load, group, source, result, stage, landing, sems):
        self.group_size, self.slack, self.load = group_size, slack, load
        self.group, self.source, self.result = group, source, result
        self.stage, self.landing, self.sems = stage, landing, sems
        self.chunks, self.pieces = result.shape[:2]
        self.levels = group.levels

    def half(self, level):
        return self.pieces >> (level + 1)

    def choice(self, chunk, level, normal):
        turned = 1 - (chunk + self.chunks - 1) // self.chunks
        return normal[level] + turned * (normal[(level + 1) % self.levels] - normal[level])

    def bit(self, chunk, level):
        return self.choice(chunk, level, self.group.bits)

    def partner(self, chunk, level):
        return self.choice(chunk, level, self.group.partners)

    def offset(self, chunk, level):
        return sum((self.bit(chunk, k) * self.half(k) for k in range(level)), 0)

    def place(self, level):
        return pl.ds(self.pieces - (self.pieces >> level), self.half(level))

    def down(self, chunk, level):
        place = self.place(level)
        return remote(
            self.stage.at[chunk, place],
            self.landing.at[chunk, place],
            self.sems,
            level,
            chunk,
            self.partner(chunk, level),
            "frames",
        )

    def up(self, chunk, level):
        done = self.result.at[chunk, pl.ds(self.offset(chunk, level + 1), self.half(level))]
        return remote(done, done, self.sems, self.levels + level, chunk, self.partner(chunk, level), "frames")

    def put(self, chunk, level):
        half = self.half(level)
        given = self.offset(chunk, level) + (1 - self.bit(chunk, level)) * half
        self.stage[chunk, self.place(level)] = self.source[chunk, pl.ds(given, half)].astype(BF)
        self.down(chunk, level).start()

    def add(self, chunk, level):
        self.down(chunk, level).wait_recv()
        kept = pl.ds(self.offset(chunk, level + 1), self.half(level))
        self.source[chunk, kept] = self.source[chunk, kept] + self.landing[chunk, self.place(level)].astype(F32)

    def advance(self, chunk, turn):
        levels = self.levels
        if turn == 0:
            if self.load is not None:
                self.load.wait(chunk)
            self.put(chunk, 0)
        elif turn < levels:
            self.add(chunk, turn - 1)
            self.put(chunk, turn)
        elif turn == levels:
            self.add(chunk, levels - 1)
            mine = pl.ds(self.offset(chunk, levels), 1)
            self.result[chunk, mine] = self.source[chunk, mine].astype(BF)
            self.up(chunk, levels - 1).start()
        else:
            self.up(chunk, 2 * levels - turn).wait_recv()
            self.up(chunk, 2 * levels - turn - 1).start()

    def tick(self, time):
        for turn in range(2 * self.levels):
            first = time - turn - (self.slack if turn else 0)

            @pl.when((first >= 0) & (first < self.chunks // self.group_size))
            def _():
                for k in range(self.group_size):
                    self.advance(first * self.group_size + k, turn)

    def last(self):
        return self.chunks // self.group_size + 2 * self.levels - 2 + self.slack

    def finish(self):
        def done(chunk, carry):
            self.up(chunk, 0).wait_recv()
            for level in range(self.levels):
                self.down(chunk, level).wait_send()
                self.up(chunk, level).wait_send()
            return carry

        lax.fori_loop(0, self.chunks, done, 0)

    @staticmethod
    def scratch(shape):
        chunks, pieces, part, width = shape
        levels = pieces.bit_length() - 1
        return [
            pltpu.VMEM((chunks, pieces - 1, part, width), BF),
            pltpu.VMEM((chunks, pieces - 1, part, width), BF),
            pltpu.SemaphoreType.DMA((2, 2 * levels, chunks)),
        ]


class SmallSum:
    def __init__(self, group, total, out, landing, sems):
        self.peers = group.everyone()
        self.total, self.out, self.landing, self.sems = total, out, landing, sems

    def copy(self, turn):
        axis, peer = self.peers[turn]
        return remote(self.out.at[turn], self.landing.at[turn], self.sems, 0, turn, peer, axis)

    def tick(self, time):
        for turn in range(len(self.peers) + 1):

            @pl.when(time == turn)
            def _():
                if turn > 0:
                    self.copy(turn - 1).wait_recv()
                    self.total[...] += self.landing[turn - 1]
                if turn < len(self.peers):
                    self.out[turn] = self.total[...]
                    self.copy(turn).start()

    def last(self):
        return len(self.peers)

    def finish(self):
        for turn in range(len(self.peers)):
            self.copy(turn).wait_send()

    @staticmethod
    def scratch(peers, shape):
        return [
            pltpu.VMEM((peers,) + shape, F32),
            pltpu.VMEM((peers,) + shape, F32),
            pltpu.SemaphoreType.DMA((2, 1, peers)),
        ]


class Bulk:
    def __init__(self, group, source, landing, sems, own_sem):
        self.group, self.source, self.landing, self.sems = group, source, landing, sems
        frame = group.frame
        self.own = pltpu.make_async_copy(source.at[frame], landing.at[frame], own_sem)

    def copy(self, far):
        other = self.group.other_frame(far)
        return remote(
            self.source.at[other], self.landing.at[self.group.frame], self.sems, 0, far - 1, other, "frames"
        )

    def start(self):
        self.own.start()
        for far in range(1, self.group.frames):
            self.copy(far).start()

    def finish(self):
        self.own.wait()
        for far in range(1, self.group.frames):
            self.copy(far).wait()

    @staticmethod
    def scratch(frames):
        return [pltpu.SemaphoreType.DMA((2, 1, frames - 1)), pltpu.SemaphoreType.DMA]


class Twice:
    def __init__(self, scatter, before):
        self.scatter, self.before = scatter, before

    def cross(self, pair):
        for k in range(2):
            self.scatter.cross(2 * pair + k + self.before)


class Move:
    def __init__(self, pairs, sems, shift=0):
        self.pairs, self.sems, self.shift = pairs, sems, shift

    def copies(self, block):
        return [
            pltpu.make_async_copy(
                src.at[block % src.shape[0]], dst.at[(block + self.shift) % dst.shape[0]], self.sems.at[k, block]
            )
            for k, (src, dst) in enumerate(self.pairs)
        ]

    def start(self, block):
        for copy in self.copies(block):
            copy.start()

    def wait(self, block):
        for copy in self.copies(block):
            copy.wait()


def pipeline(phases, steps=0, beside=None):
    def step(i, carry):
        for lag in (0, 1, 2, LAG):
            first = 0
            for blocks, gathers, scatters, compute, take in phases:
                block = i - lag - first
                first += blocks

                @pl.when((block >= 0) & (block < blocks))
                def _():
                    if lag == 0:
                        for gather in gathers:
                            gather.forward(block)
                    elif lag == 1:
                        for gather in gathers:
                            gather.arrive(block)
                        compute(block)
                    elif lag == 2:
                        for scatter, before in scatters:
                            scatter.cross(block + before)
                    elif take is not None:
                        take(block)

        if beside is not None:
            beside(i)
        return carry

    lax.fori_loop(0, max(sum(phase[0] for phase in phases) + LAG, steps), step, 0)
    for scatter in {id(scatter): scatter for phase in phases for scatter, _ in phase[2]}.values():
        if isinstance(scatter, Scatter):
            scatter.finish()


def coded_rows(codes_ref, block, actions):
    return (lax.broadcasted_iota(jnp.int32, (actions, 1), 0) == codes_ref[0, block]).astype(F32)


def space_stream(stream_ref, codes_ref, table_ref, block):
    hot = coded_rows(codes_ref, block, table_ref.shape[0])
    added = jnp.sum(hot * table_ref[...].astype(F32), axis=0, keepdims=True)
    return stream_ref[block].astype(F32) + added


def row_of(gain_ref):
    return gain_ref[...].astype(F32)[None]


def attention_block(whole_ref, w_qkv_ref, w_out_ref, qkv_ref, att_ref, seen_ref):
    _, part, width = whole_ref.shape
    normed = whole_ref[...].reshape(4 * part, width)
    for member in range(3):
        qkv_ref[member] = dot(normed, w_qkv_ref[member], (1, 0)).astype(BF)
    att_ref[...] = attend(qkv_ref[0], qkv_ref[1], qkv_ref[2], seen_ref)
    return dot(att_ref[...], w_out_ref[...], (1, 0))


def each_block(blocks, work):
    def one(block, carry):
        work(block)
        return carry

    lax.fori_loop(0, blocks, one, 0)


def call(kernel, name, collective_id, operands, outs, scratch, flops):
    def specs(items):
        return [pl.BlockSpec(memory_space=space) for _, space in items]

    return pl.pallas_call(
        kernel,
        name=name,
        out_shape=[shape for shape, _ in outs],
        in_specs=specs(operands),
        out_specs=specs(outs),
        scratch_shapes=scratch,
        compiler_params=pltpu.CompilerParams(
            collective_id=collective_id, has_side_effects=True, vmem_limit_bytes=LIMIT
        ),
        cost_estimate=pl.CostEstimate(flops=flops, bytes_accessed=16 << 20, transcendentals=0),
    )(*(array for array, _ in operands))


def inside(*items):
    return [(item, pltpu.VMEM) for item in items]


def outside(*items):
    return [(item, pl.ANY) for item in items]


def scalars(item):
    return [(item, pltpu.SMEM)]


def held_like(shapes):
    return [pltpu.VMEM(shape.shape, shape.dtype) for shape in shapes] + [
        pltpu.SemaphoreType.DMA((len(shapes), shapes[0].shape[0]))
    ]


def saved_shapes(blocks, part, width, inner):
    return [
        jax.ShapeDtypeStruct((blocks, 4, part, width), BF),
        jax.ShapeDtypeStruct((blocks, 3, 4 * part, inner), BF),
        jax.ShapeDtypeStruct((blocks, 4 * part, inner), BF),
    ]


def backward_kernel(
    frames,
    grad_ref,
    stream_ref,
    tokens_ref,
    codes_ref,
    table_ref,
    gain_sp_ref,
    gain_tm_ref,
    gain_ff_out,
    w_qkv_sp_ref,
    w_out_sp_ref,
    w_qkv_tm_ref,
    w_out_tm_ref,
    *refs,
):
    time_saved, space_saved, refs = refs[:3], refs[3:6], refs[6:]
    rest_in, mixed_ref, out_ref, space_total, time_total, rest_total, small_ref, mixed_out_ref, *refs = refs
    small_clips, seen_ref, mixed_sems, own_sem, stage, stage_sems, landing, *refs = refs
    slots, refs = refs[:3], refs[3:]
    time_load_sems, space_load_sems, rest_load_sems, w_sum, shared_sum, *refs = refs
    grad_whole_ref, packed_ref, time_sems, space_sems, *refs = refs
    whole_ref, qkv_ref, att_ref = slots
    blocks, _, part, width = grad_whole_ref.shape
    rows = 4 * part
    group = Group(frames, True)
    group.meet()
    time_gather = Gather(group, grad_whole_ref, time_sems)
    space_gather = Gather(group, grad_whole_ref, space_sems)
    scatter = Scatter(group, *refs[:6])
    rest_load = Move([(rest_in, shared_sum)], rest_load_sems)
    rest_reduce = Reduce(2, 1, rest_load, group, shared_sum, rest_total, *refs[6:9])
    time_reduce = Reduce(2, 1, None, group, w_sum, time_total, *refs[9:12])
    space_reduce = Reduce(1, 0, None, group, shared_sum, space_total, *refs[6:8], refs[12])
    small = SmallSum(group, small_ref, *refs[13:])
    exchange = Exchange(group, stage, landing, stage_sems)
    mixed_bulk = Bulk(group, mixed_ref, mixed_out_ref, mixed_sems, own_sem)
    time_load = Move(list(zip(time_saved, slots)), time_load_sems)
    space_load = Move(list(zip(space_saved, slots)), space_load_sems, blocks)
    ahead = whole_ref.shape[0] - 1

    def gather_grad(gather, block, grad):
        grad_whole_ref[block, group.me] = grad.astype(BF)
        gather.start(block)

    each_block(blocks, lambda block: gather_grad(time_gather, block, grad_ref[block]))
    each_block(ahead, time_load.start)
    each_block(CHUNKS, rest_load.start)
    mixed_bulk.start()
    w_sum[...] = jnp.zeros_like(w_sum)
    seen_ref[...] = visible(rows, frames, 1).astype(F32)
    small_ref[...] = jnp.zeros_like(small_ref)
    small_ref[10:11, :] = gain_ff_out[...]

    def back(block, at, w_qkv_ref):
        scatter.free(at)
        scatter.send(at, sum(dot(packed_ref[block, member], w_qkv_ref[member], (1, 1)) for member in range(3)))

    def attention(block, slot, w_out_ref, sums, seen):
        grad_y = grad_whole_ref[block].reshape(rows, width)
        grad_att = dot(grad_y, w_out_ref[...], (1, 1)).astype(BF)
        grads = attend_back(qkv_ref[slot, 0], qkv_ref[slot, 1], qkv_ref[slot, 2], grad_att, seen)
        for member in range(3):
            packed_ref[block, member] = grads[member]
        piece = sums.shape[1:]
        normed = whole_ref[slot].reshape(rows, width)
        quarter = width // 4
        for member in range(4):
            small = packed_ref[block, member] if member < 3 else att_ref[slot]
            wide = normed if member < 3 else grad_y
            grad_w = dot(small, wide, (0, 0))
            cuts = [grad_w[:, k * quarter : (k + 1) * quarter] for k in range(4)]
            for k in range(2):
                sums[2 * member + k] += jnp.concatenate(cuts[2 * k : 2 * k + 2], axis=0).reshape(piece)

    def time_compute(block):
        time_load.wait(block)

        @pl.when(block + ahead < blocks)
        def _():
            time_load.start(block + ahead)

        @pl.when(block + ahead >= blocks)
        def _():
            space_load.start(block + ahead - blocks)

        attention(block, block % (ahead + 1), w_out_tm_ref, w_sum, seen_ref)
        time_gather.sent(block)
        back(block, block, w_qkv_tm_ref)

    def time_take(block):
        stream = unpack(stream_ref[block], width)
        grad_part, grad_gain = norm_backward(scatter.take(block), stream, row_of(gain_tm_ref))
        exchange.push(block, grad_ref[block] + grad_part)
        small_ref[9:10, :] += grad_gain

    def space_compute(block):
        space_load.wait(block)

        @pl.when(block + ahead < blocks)
        def _():
            space_load.start(block + ahead)

        attention(block, (block + blocks) % (ahead + 1), w_out_sp_ref, shared_sum, None)

    def space_back(pair):
        for k in range(2):
            back(2 * pair + k, 2 * pair + k + blocks, w_qkv_sp_ref)

    def space_take(pair):
        for k in range(2):
            block = 2 * pair + k
            stream = space_stream(tokens_ref, codes_ref, table_ref, block)
            grad_part, grad_gain = norm_backward(scatter.take(block + blocks), stream, row_of(gain_sp_ref))
            grad_stream = unpack(landing[block], width) + grad_part
            out_ref[block] = grad_stream
            small_ref[8:9, :] += grad_gain
            small_clips[pl.ds(block, 1)] = jnp.sum(grad_stream, axis=0, keepdims=True)[None]

    launch_lag = LAG + 2
    space_first = blocks + GAP
    space_done = space_first + blocks
    taken = space_done + blocks // 2 + LAG - 1

    def beside(i):
        block = i - launch_lag

        @pl.when((block >= 0) & (block < blocks))
        def _():
            exchange.arrive(block)
            gather_grad(space_gather, block, unpack(landing[block], width))

        rest_reduce.tick(i)
        time_reduce.tick(i - blocks)

        @pl.when(i == space_first)
        def _():
            shared_sum[...] = jnp.zeros_like(shared_sum)

        @pl.when(i == space_done - 1)
        def _():
            rest_reduce.finish()

        space_reduce.tick(i - space_done)

        @pl.when(i == taken)
        def _():
            for clip in range(blocks):
                small_ref[0:8, :] += coded_rows(codes_ref, clip, 8) * small_clips[clip]

        small.tick(i - taken)

    pipeline(
        [
            (blocks, [time_gather], [(scatter, 0)], time_compute, time_take),
            (GAP, [], [], lambda block: None, None),
            (blocks, [space_gather], [], space_compute, None),
            (blocks // 2, [], [(Twice(scatter, blocks), 0)], space_back, space_take),
        ],
        max(space_done + space_reduce.last() + 1, taken + small.last() + 1),
        beside,
    )
    each_block(blocks, space_gather.sent)
    each_block(blocks, exchange.sent)
    for moved in (time_reduce, space_reduce, small, mixed_bulk):
        moved.finish()


def backward(frames, grad, stream, tokens, codes, table, gains, weights, kept, rest_sum, mixed):
    blocks, part, width = tokens.shape
    inner = weights[1].shape[0]
    rows = 4 * part
    packed = packed_shape(blocks, frames, part, width)
    sums = (CHUNKS, frames, 2 * inner // frames, width // 4)
    small = (16, width)
    peers = 2 + frames.bit_length() - 1
    reduce = Reduce.scratch(sums)
    return call(
        functools.partial(backward_kernel, frames),
        "backward",
        2,
        inside(grad, stream, tokens)
        + scalars(codes)
        + inside(table, *gains, *weights)
        + outside(*kept, rest_sum, mixed),
        inside(jax.ShapeDtypeStruct(tokens.shape, F32))
        + inside(*[jax.ShapeDtypeStruct(sums, BF)] * 3, jax.ShapeDtypeStruct(small, F32))
        + outside(jax.ShapeDtypeStruct(mixed.shape, BF)),
        [pltpu.VMEM((blocks, 1, width), F32), pltpu.VMEM((rows, rows), F32)]
        + Bulk.scratch(frames)
        + Exchange.scratch(packed)
        + [pltpu.VMEM(packed, BF)]
        + [pltpu.VMEM((3,) + each.shape[1:], BF) for each in kept[:3]]
        + [pltpu.SemaphoreType.DMA((3, blocks))] * 2
        + [pltpu.SemaphoreType.DMA((1, CHUNKS)), pltpu.VMEM(sums, F32), pltpu.VMEM(sums, F32)]
        + [pltpu.VMEM((blocks, 4, part, width), BF), pltpu.VMEM((blocks, 3, rows, inner), BF)]
        + [Gather.scratch(blocks)] * 2
        + Scatter.scratch(2 * blocks, blocks, part, width)
        + reduce
        + reduce
        + reduce[2:]
        + SmallSum.scratch(peers, small),
        1 << 30,
    )


def gelu_parts(hidden):
    slope = 0.7978845608028654
    square = hidden * hidden
    bent = jnp.tanh(slope * hidden * (1.0 + 0.044715 * square))
    half = 0.5 * (1.0 + bent)
    grad = half + 0.5 * hidden * (1.0 - bent * bent) * (slope * (1.0 + 3 * 0.044715 * square))
    return hidden * half, grad


def forward_kernel(
    frames,
    tokens_ref,
    codes_ref,
    table_ref,
    cot_in,
    gain_sp_ref,
    gain_tm_ref,
    gain_ff_ref,
    w_qkv_sp_ref,
    w_out_sp_ref,
    w_qkv_tm_ref,
    w_out_tm_ref,
    w_up_in,
    w_down_in,
    stream_ref,
    mixed_ref,
    grad_ref,
    gain_out_ref,
    total_ref,
    sum_out,
    *refs,
):
    space_saved, time_saved, refs = refs[:3], refs[3:6], refs[6:]
    w_sum, rest_sum, sum_sems, w_up_ref, w_down_ref, w_sems, *refs = refs
    whole_ref, qkv_ref, att_ref, space_sems, time_sems, seen_ref, stage, stage_sems, *refs = refs
    cot_ref, bulk_sems, own_sem, cot_whole_ref, sp_sems, tm_sems, ffn_sems, cot_sems, *refs = refs
    blocks, _, part, width = whole_ref.shape
    rows = 4 * part
    half = w_up_ref.shape[2] // 2
    group = Group(frames, True)
    group.meet()
    space_gather = Gather(group, whole_ref, sp_sems)
    time_gather = Gather(group, whole_ref, tm_sems)
    ffn_gather = Gather(group, whole_ref, ffn_sems)
    cot_gather = Gather(group, cot_whole_ref, cot_sems)
    scatter = Scatter(group, *refs[:6])
    grad_scatter = Scatter(group, *refs[6:12])
    reduce = Reduce(2, 1, None, group, w_sum, total_ref, *refs[12:])
    exchange = Exchange(group, stage, stream_ref, stage_sems)
    cot_bulk = Bulk(group, cot_in, cot_ref, bulk_sems, own_sem)
    w_load = Move([(w_up_in, w_up_ref), (w_down_in, w_down_ref)], w_sems)
    sum_save = Move([(rest_sum, sum_out)], sum_sems)

    def gather_normed(gather, block, stream, gain_ref):
        unit, _ = norm_parts(stream)
        whole_ref[block, group.me] = (unit * row_of(gain_ref)).astype(BF)
        gather.start(block)

    def begin(block):
        gather_normed(space_gather, block, space_stream(tokens_ref, codes_ref, table_ref, block), gain_sp_ref)

    each_block(blocks, begin)
    cot_bulk.start()
    w_load.start(0)
    seen_ref[...] = visible(rows, frames).astype(F32)
    w_sum[...] = jnp.zeros_like(w_sum)
    rest_sum[...] = jnp.zeros_like(rest_sum)
    gain_out_ref[...] = jnp.zeros_like(gain_out_ref)

    def attention(block, gather, saved, sems, w_qkv_ref, w_out_ref, seen, at):
        whole_save = Move([(whole_ref, saved[0])], sems.at[0:1])
        save = Move([(qkv_ref, saved[1]), (att_ref, saved[2])], sems.at[1:3])
        whole_save.start(block)

        @pl.when(block >= 2)
        def _():
            save.wait(block - 2)

        slot = block % 2
        result = attention_block(whole_ref.at[block], w_qkv_ref, w_out_ref, qkv_ref.at[slot], att_ref.at[slot], seen)
        save.start(block)
        gather.sent(block)
        whole_save.wait(block)
        scatter.free(at)
        scatter.send(at, result)

        @pl.when(block == blocks - 1)
        def _():
            save.wait(blocks - 2)
            save.wait(blocks - 1)

    def space_compute(block):
        attention(block, space_gather, space_saved, space_sems, w_qkv_sp_ref, w_out_sp_ref, None, block)

    def time_compute(block):
        at = block + blocks
        attention(block, time_gather, time_saved, time_sems, w_qkv_tm_ref, w_out_tm_ref, seen_ref, at)

    def space_take(block):
        exchange.push(block, space_stream(tokens_ref, codes_ref, table_ref, block) + scatter.take(block))

    def time_take(block):
        stream = unpack(stream_ref[block], width) + scatter.take(block + blocks)
        grad_ref[block] = stream
        gather_normed(ffn_gather, block, stream, gain_ff_ref)
        cot_whole_ref[block, group.me] = unpack(cot_ref[:, block], width).astype(BF)
        cot_gather.start(block)

    def ffn_compute(block, second):
        sums = rest_sum if second else w_sum
        hidden = pl.ds(half if second else 0, half)
        normed = whole_ref[block].reshape(rows, width)
        grad_y = cot_whole_ref[block].reshape(rows, width)
        w_up = w_up_ref[0, :, hidden]
        w_down = w_down_ref[0, hidden, :]
        activated, slope = gelu_parts(dot(normed, w_up, (1, 0)))
        activated = activated.astype(BF)
        grad_pre = (dot(grad_y, w_down, (1, 1)) * slope).astype(BF)
        if not second:
            scatter.free(block + 2 * blocks)
        for each, at, values in (
            (scatter, block + 2 * blocks, dot(activated, w_down, (1, 0))),
            (grad_scatter, block, dot(grad_pre, w_up, (1, 1))),
        ):
            if second:
                each.send(at, values, True)
            else:
                each.put(at, values)
        for first, small, wide in ((0, grad_pre, normed), (4, activated, grad_y)):
            grad_w = dot(small, wide, (0, 0))
            for k in range(4):
                cut = grad_w[:, k * (width // 4) : (k + 1) * (width // 4)]
                sums[first + k] += cut.reshape(sums.shape[1:])

    def take(block):
        stream = grad_ref[block]
        for frame, piece in enumerate(pack(stream + scatter.take(block + 2 * blocks), frames)):
            mixed_ref[frame, block] = piece.astype(BF)
        grad_part, grad_gain = norm_backward(grad_scatter.take(block), stream, row_of(gain_ff_ref))
        grad_ref[block] = cot_whole_ref[block, group.me].astype(F32) + grad_part
        gain_out_ref[...] += grad_gain

    launch_lag = LAG + 2
    ffn_first = 2 * blocks + GAP

    def beside(i):
        block = i - launch_lag

        @pl.when((block >= 0) & (block < blocks))
        def _():
            exchange.arrive(block)
            gather_normed(time_gather, block, unpack(stream_ref[block], width), gain_tm_ref)

        @pl.when(i == blocks + GAP)
        def _():
            cot_bulk.finish()

        @pl.when(i == ffn_first)
        def _():
            w_load.wait(0)

        reduce.tick(i - ffn_first - blocks)

        @pl.when(i == ffn_first + 2 * blocks)
        def _():
            each_block(CHUNKS, sum_save.start)

    pipeline(
        [
            (blocks, [space_gather], [(scatter, 0)], space_compute, space_take),
            (GAP, [], [], lambda block: None, None),
            (blocks, [time_gather], [(scatter, blocks)], time_compute, time_take),
            (blocks, [ffn_gather, cot_gather], [], lambda block: ffn_compute(block, False), None),
            (blocks, [], [(scatter, 2 * blocks), (grad_scatter, 0)], lambda block: ffn_compute(block, True), take),
        ],
        ffn_first + blocks + reduce.last() + 1,
        beside,
    )
    each_block(blocks, ffn_gather.sent)
    each_block(blocks, cot_gather.sent)
    each_block(blocks, exchange.sent)
    reduce.finish()
    each_block(CHUNKS, sum_save.wait)


def forward(frames, tokens, codes, table, cot, gains, w_qkv_sp, w_out_sp, w_qkv_tm, w_out_tm, w_up, w_down):
    blocks, part, width = tokens.shape
    inner = w_out_sp.shape[0]
    packed = packed_shape(blocks, frames, part, width)
    whole = pltpu.VMEM((blocks, 4, part, width), BF)
    saved = saved_shapes(blocks, part, width, inner)
    sums = jax.ShapeDtypeStruct((CHUNKS, frames, w_up.shape[1] // (2 * frames), width // 4), F32)
    weights = [w_up[None], w_down[None]]
    return call(
        functools.partial(forward_kernel, frames),
        "forward_and_ffn",
        1,
        inside(tokens)
        + scalars(codes)
        + inside(table)
        + outside(cot)
        + inside(*gains, w_qkv_sp, w_out_sp, w_qkv_tm, w_out_tm)
        + outside(*weights),
        inside(
            jax.ShapeDtypeStruct(packed, BF),
            jax.ShapeDtypeStruct(cot.shape, BF),
            jax.ShapeDtypeStruct((blocks, part, width), F32),
            jax.ShapeDtypeStruct((1, width), F32),
            jax.ShapeDtypeStruct(sums.shape, BF),
        )
        + outside(sums, *saved, *saved),
        [pltpu.VMEM(sums.shape, F32), pltpu.VMEM(sums.shape, F32), pltpu.SemaphoreType.DMA((1, CHUNKS))]
        + held_like(weights)
        + [
            whole,
            pltpu.VMEM((2,) + saved[1].shape[1:], BF),
            pltpu.VMEM((2,) + saved[2].shape[1:], BF),
            pltpu.SemaphoreType.DMA((3, blocks)),
            pltpu.SemaphoreType.DMA((3, blocks)),
            pltpu.VMEM((4 * part, 4 * part), F32),
        ]
        + Exchange.scratch(packed)
        + [pltpu.VMEM(cot.shape, BF)]
        + Bulk.scratch(frames)
        + [whole]
        + [Gather.scratch(blocks)] * 4
        + Scatter.scratch(3 * blocks, blocks, part, width)
        + Scatter.scratch(blocks, blocks, part, width)
        + Reduce.scratch(sums.shape),
        (16 * inner + 12 * w_up.shape[1]) * blocks * 4 * part * width,
    )


def widen_kernel(frames, space_ref, time_ref, first_ref, second_ref, mixed_ref, small_ref, *outs):
    step = pl.program_id(0)
    mixed_out, table_out, *gain_outs = outs[:5]
    for sums_ref, qkv_out, w_out_out in ((space_ref, *outs[5:7]), (time_ref, *outs[7:9])):
        quarter = sums_ref.shape[3]

        @pl.when(step < 3)
        def _():
            for k in range(4):
                qkv_out[0, k * quarter : (k + 1) * quarter] = sums_ref[k // 2, k % 2].astype(F32).T

        @pl.when(step == 3)
        def _():
            for k in range(4):
                w_out_out[:, k * quarter : (k + 1) * quarter] = sums_ref[k // 2, k % 2].astype(F32)

    up_out, down_out = outs[9:]

    @pl.when(step < 2)
    def _():
        for k, ffn_ref in enumerate((first_ref, second_ref)):
            _, hidden, quarter = ffn_ref.shape
            for c in range(2):
                rows, cols = pl.ds(c * quarter, quarter), pl.ds(k * hidden, hidden)
                up_out[rows, cols] = ffn_ref[c].astype(F32).T

    @pl.when(step >= 2)
    def _():
        for k, ffn_ref in enumerate((first_ref, second_ref)):
            _, hidden, quarter = ffn_ref.shape
            for c in range(2):
                rows, cols = pl.ds(k * hidden, hidden), pl.ds(c * quarter, quarter)
                down_out[rows, cols] = ffn_ref[c].astype(F32)

    for block in range(mixed_ref.shape[1]):
        mixed_out[block] = unpack(mixed_ref[:, block], mixed_out.shape[2]).astype(BF)

    @pl.when(step == 0)
    def _():
        table_out[...] = small_ref[0:8, :]
        for k, gain_out in enumerate(gain_outs):
            gain_out[...] = small_ref[8 + k : 9 + k, :]


def widen(frames, space_sums, time_sums, first_sums, second_sums, mixed, small, part, inner):
    width = small.shape[1]
    half = width // 2
    blocks = mixed.shape[1]
    hidden = 2 * first_sums.shape[1] * first_sums.shape[2]
    last_qkv = lambda i: (jnp.minimum(i, 2), 0, 0)
    whole = lambda i: (0, 0)
    turned = [
        (jax.ShapeDtypeStruct((3, width, inner), F32), pl.BlockSpec((1, width, inner), last_qkv)),
        (jax.ShapeDtypeStruct((inner, width), F32), pl.BlockSpec((inner, width), whole)),
    ]
    outs = [
        (jax.ShapeDtypeStruct((blocks, part, width), BF), pl.BlockSpec((blocks // 4, part, width), lambda i: (i, 0, 0))),
        (jax.ShapeDtypeStruct((8, width), F32), pl.BlockSpec((8, width), whole)),
    ]
    outs += [(jax.ShapeDtypeStruct((1, width), F32), pl.BlockSpec((1, width), whole))] * 3 + turned + turned
    outs += [
        (jax.ShapeDtypeStruct((width, hidden), F32), pl.BlockSpec((half, hidden), lambda i: (jnp.minimum(i, 1), 0))),
        (
            jax.ShapeDtypeStruct((hidden, width), F32),
            pl.BlockSpec((hidden, half), lambda i: (0, jnp.maximum(i - 2, 0))),
        ),
    ]
    quarter = width // 4
    chunk = pl.BlockSpec((2, 2, inner, quarter), lambda i: (i, 0, 0, 0))
    ffn_chunk = pl.BlockSpec((2, hidden // 2, quarter), lambda i: (i, 0, 0))
    return pl.pallas_call(
        functools.partial(widen_kernel, frames),
        name="widen",
        grid=(4,),
        out_shape=[shape for shape, _ in outs],
        in_specs=[
            chunk,
            chunk,
            ffn_chunk,
            ffn_chunk,
            pl.BlockSpec((frames, blocks // 4) + mixed.shape[2:], lambda i: (0, i, 0, 0)),
            pl.BlockSpec(small.shape, whole),
        ],
        out_specs=[spec for _, spec in outs],
        compiler_params=pltpu.CompilerParams(vmem_limit_bytes=LIMIT),
    )(
        space_sums.reshape(CHUNKS, 2, inner, quarter),
        time_sums.reshape(CHUNKS, 2, inner, quarter),
        first_sums.reshape(CHUNKS, hidden // 2, quarter),
        second_sums.reshape(CHUNKS, hidden // 2, quarter),
        mixed,
        small,
    )


def pack_rows(values, frames):
    blocks, part, width = values.shape
    shape = packed_shape(blocks, frames, part, width)
    cut = values.reshape(blocks, frames, part // frames, width // shape[-1], shape[-1])
    return cut.transpose(1, 0, 3, 2, 4).reshape((frames, blocks) + shape[2:])


def body(
    frames,
    tokens,
    codes,
    table,
    gain_space,
    gain_time,
    gain_ffn,
    w_qkv_space,
    w_out_space,
    w_qkv_time,
    w_out_time,
    w_up,
    w_down,
    cotangent,
):
    gain_sp, gain_tm, gain_ff = gain_space, gain_time, gain_ffn
    w_qkv_sp = w_qkv_space.swapaxes(0, 1)
    w_qkv_tm = w_qkv_time.swapaxes(0, 1)
    _, blocks, part, width = tokens.shape

    gains = gain_sp, gain_tm, gain_ff
    weights = w_qkv_sp, w_out_space, w_qkv_tm, w_out_time, w_up, w_down
    stream_one, mixed, grad_two, grad_gain_ff, first_totals, ffn_sums, *kept = forward(
        frames, tokens[0], codes, table, pack_rows(cotangent[0], frames), gains, *weights
    )
    grad_zero, space_totals, time_totals, ffn_totals, small, mixed = backward(
        frames,
        grad_two,
        stream_one,
        tokens[0],
        codes,
        table,
        (gain_sp, gain_tm, grad_gain_ff),
        weights[:4],
        kept[3:] + kept[:3],
        ffn_sums,
        mixed,
    )
    mixed, grad_tab, gain_sp, gain_tm, gain_ff, *grads = widen(
        frames, space_totals, time_totals, first_totals, ffn_totals, mixed, small, part, w_out_space.shape[0]
    )
    return (
        mixed[None],
        grad_zero[None],
        grad_tab,
        gain_sp[0],
        gain_tm[0],
        gain_ff[0],
        grads[0].swapaxes(0, 1),
        grads[1],
        grads[2].swapaxes(0, 1),
        grads[3],
        *grads[4:],
    )


def solution(mesh):
    rows = P("frames", None, "tensor", None)
    return jax.shard_map(
        functools.partial(body, mesh.shape["frames"]),
        mesh=mesh,
        in_specs=(
            rows,
            P("frames", None),
            P(),
            P(),
            P(),
            P(),
            P(None, None, "tensor"),
            P("tensor", None),
            P(None, None, "tensor"),
            P("tensor", None),
            P(None, "tensor"),
            P("tensor", None),
            rows,
        ),
        out_specs=(
            rows,
            rows,
            P(),
            P(),
            P(),
            P(),
            P(None, None, "tensor"),
            P("tensor", None),
            P(None, None, "tensor"),
            P("tensor", None),
            P(None, "tensor"),
            P("tensor", None),
        ),
        check_vma=False,
    )
```

```python
import functools

import jax
import jax.numpy as jnp
from jax import lax
from jax.experimental import pallas as pl
from jax.experimental.pallas import tpu as pltpu
from jax.sharding import PartitionSpec as P

HD = 64
EPS = 1e-06
BF = jnp.bfloat16
F32 = jnp.float32
MESH = pl.DeviceIdType.MESH
LIMIT = 63 * 1024 * 1024
LAG = 5
GAP = 2
CHUNKS = 8


def dot(left, right, contract):
    return lax.dot_general(left, right, ((contract[:1], contract[1:]), ((), ())), preferred_element_type=F32)


def norm_parts(values):
    factor = lax.rsqrt(jnp.mean(values * values, axis=-1, keepdims=True) + EPS)
    return values * factor, factor


def norm_backward(grad_normed, stream, gain_vec):
    unit, factor = norm_parts(stream)
    scaled = grad_normed * gain_vec
    grad_stream = (scaled - unit * jnp.mean(scaled * unit, axis=-1, keepdims=True)) * factor
    return grad_stream, jnp.sum(grad_normed * unit, axis=0, keepdims=True)


def head_mask(rows, width, head):
    lane = lax.broadcasted_iota(jnp.int32, (rows, width), 1)
    return (lane >= head * HD) & (lane < (head + 1) * HD)


def visible(rows, frames, query_dim=0):
    part = rows // 4
    spots = part // frames
    row = lax.broadcasted_iota(jnp.int32, (rows, rows), query_dim)
    col = lax.broadcasted_iota(jnp.int32, (rows, rows), 1 - query_dim)
    same_part = row // part == col // part
    same_spot = row % spots == col % spots
    earlier = (col % part) // spots <= (row % part) // spots
    return same_part & same_spot & earlier


def block_probs(queries, keys_in, seen):
    scores = dot(queries, keys_in, (1, 1))
    if seen is not None:
        scores = jnp.where(seen[...] > 0, scores, -1e30)
    raised = jnp.exp(scores - jnp.max(scores, axis=-1, keepdims=True))
    return raised * (1.0 / jnp.sum(raised, axis=-1, keepdims=True))


def attend(queries, keys_in, values, seen):
    rows, width = queries.shape
    total = jnp.zeros((rows, width), F32)
    queries = queries * BF(HD ** (-0.5))
    for head in range(width // HD):
        mine = head_mask(rows, width, head)
        probs = block_probs(jnp.where(mine, queries, 0), keys_in, seen)
        total = total + dot(probs.astype(BF), jnp.where(mine, values, 0), (1, 0))
    return total.astype(BF)


def attend_back(queries, keys_in, values, grad_att, seen):
    rows, width = queries.shape
    zero = jnp.zeros((rows, width), F32)
    grad_q, grad_k, grad_v = zero, zero, zero
    scale = BF(HD ** (-0.5))
    queries = queries * scale
    scaled_keys = keys_in * scale
    for head in range(width // HD):
        mine = head_mask(rows, width, head)
        my_queries = jnp.where(mine, queries, 0)
        my_grad = jnp.where(mine, grad_att, 0)
        scores = dot(keys_in, my_queries, (1, 1))
        if seen is not None:
            scores = jnp.where(seen[...] > 0, scores, -1e30)
        raised = jnp.exp(scores - jnp.max(scores, axis=0, keepdims=True))
        probs = raised * (1.0 / jnp.sum(raised, axis=0, keepdims=True))
        grad_probs = dot(values, my_grad, (1, 1))
        row_dot = jnp.sum(grad_probs * probs, axis=0, keepdims=True)
        grad_scores = (probs * (grad_probs - row_dot)).astype(BF)
        grad_q = grad_q + dot(grad_scores, jnp.where(mine, scaled_keys, 0), (0, 0))
        grad_k = grad_k + dot(grad_scores, my_queries, (1, 0))
        grad_v = grad_v + dot(probs.astype(BF), my_grad, (1, 0))
    return grad_q.astype(BF), grad_k.astype(BF), grad_v.astype(BF)


class Group:
    def __init__(self, frames=1, all_frames=False):
        me = lax.axis_index("tensor")
        self.x, self.c = me // 2, me % 2
        self.me = me
        self.chip_peer = 2 * (1 - self.x) + self.c
        self.core_peer = 2 * self.x + 1 - self.c
        self.levels = frames.bit_length() - 1
        self.bits, self.partners = [], []
        self.frames, self.all_frames = frames, all_frames
        self.frame = frame = lax.axis_index("frames")
        for level in range(self.levels):
            bit = (frame // 2**level) % 2
            self.bits.append(bit)
            self.partners.append(frame + (1 - 2 * bit) * 2**level)

    def everyone(self):
        return [("tensor", self.chip_peer), ("tensor", self.core_peer)] + [
            ("frames", partner) for partner in self.partners
        ]

    def other_frame(self, distance):
        return (self.frame + distance) % self.frames

    def meet(self):
        barrier = pltpu.get_barrier_semaphore()
        peers = self.everyone()
        if self.all_frames:
            peers = peers[:2] + [("frames", self.other_frame(far)) for far in range(1, self.frames)]
        for axis, peer in peers:
            pl.semaphore_signal(barrier, inc=1, device_id={axis: peer}, device_id_type=MESH)
        pl.semaphore_wait(barrier, len(peers))


def remote(src, dst, sems, kind, block, peer, axis="tensor"):
    return pltpu.make_async_remote_copy(
        src_ref=src,
        dst_ref=dst,
        send_sem=sems.at[0, kind, block],
        recv_sem=sems.at[1, kind, block],
        device_id={axis: peer},
        device_id_type=MESH,
    )


class Gather:
    def __init__(self, group, whole, sems):
        self.group, self.whole, self.sems = group, whole, sems

    def copy(self, kind, block):
        g = self.group
        quarter = self.whole.at[block, g.chip_peer if kind == 2 else g.me]
        return remote(quarter, quarter, self.sems, kind, block, g.chip_peer if kind == 0 else g.core_peer)

    def start(self, block):
        self.copy(0, block).start()
        self.copy(1, block).start()

    def forward(self, block):
        self.copy(0, block).wait_recv()
        self.copy(2, block).start()

    def arrive(self, block):
        self.copy(1, block).wait_recv()
        self.copy(2, block).wait_recv()

    def sent(self, block):
        for kind in range(3):
            self.copy(kind, block).wait_send()

    @staticmethod
    def scratch(blocks):
        return pltpu.SemaphoreType.DMA((2, 3, blocks))


class Scatter:
    def __init__(self, group, kept, near_out, near_in, far_out, far_in, sems):
        self.group, self.kept, self.sems = group, kept, sems
        self.near_out, self.near_in, self.far_out, self.far_in = near_out, near_in, far_out, far_in
        self.slots, self.blocks = near_out.shape[0], sems.shape[2]

    def near(self, block):
        slot = block % self.slots
        return remote(self.near_out.at[slot], self.near_in.at[slot], self.sems, 0, block, self.group.core_peer)

    def far(self, block):
        slot = block % self.slots
        return remote(self.far_out.at[slot], self.far_in.at[slot], self.sems, 1, block, self.group.chip_peer)

    def free(self, block):
        if self.blocks > self.slots:

            @pl.when(block >= self.slots)
            def _():
                self.near(block - self.slots).wait_send()
                self.far(block - self.slots).wait_send()

    def put(self, block, values, more=False):
        slot = block % self.slots
        for x in range(2):
            first, second = (values[(2 * x + c) * self.part : (2 * x + c + 1) * self.part] for c in range(2))
            own = jnp.where(self.group.c == 0, first, second)
            given = jnp.where(self.group.c == 0, second, first)
            if more:
                own = own + self.kept[slot, x]
                given = given + self.near_out[slot, x].astype(F32)
            self.kept[slot, x] = own
            self.near_out[slot, x] = given.astype(BF)

    def send(self, block, values, more=False):
        self.put(block, values, more)
        self.near(block).start()

    @property
    def part(self):
        return self.kept.shape[2]

    def cross(self, block):
        x, slot = 1 - self.group.x, block % self.slots
        self.near(block).wait_recv()
        self.far_out[slot] = (self.kept[slot, x] + self.near_in[slot, x].astype(F32)).astype(BF)
        self.far(block).start()

    def take(self, block):
        x, slot = self.group.x, block % self.slots
        self.far(block).wait_recv()
        return self.kept[slot, x] + self.near_in[slot, x].astype(F32) + self.far_in[slot].astype(F32)

    def finish(self):
        def sent(block, carry):
            self.near(block).wait_send()
            self.far(block).wait_send()
            return carry

        lax.fori_loop(self.blocks - self.slots, self.blocks, sent, 0)

    @staticmethod
    def scratch(blocks, slots, part, width):
        return [
            pltpu.VMEM((slots, 2, part, width), F32),
            pltpu.VMEM((slots, 2, part, width), BF),
            pltpu.VMEM((slots, 2, part, width), BF),
            pltpu.VMEM((slots, part, width), BF),
            pltpu.VMEM((slots, part, width), BF),
            pltpu.SemaphoreType.DMA((2, 2, blocks)),
        ]


def packed_shape(blocks, frames, part, width):
    spots = part // frames
    cuts = max(1, 16 // spots)
    return (blocks, frames, cuts * spots, width // cuts)


def pack(values, frames):
    rows, width = values.shape
    spots = rows // frames
    cuts = max(1, 16 // spots)
    wide = width // cuts
    return [
        jnp.concatenate(
            [values[frame * spots : (frame + 1) * spots, k * wide : (k + 1) * wide] for k in range(cuts)], axis=0
        )
        for frame in range(frames)
    ]


def unpack(packed, width):
    frames, rows, wide = packed.shape
    cuts = width // wide
    spots = rows // cuts
    packed = packed.astype(F32)
    return jnp.concatenate(
        [
            jnp.concatenate([packed[frame, k * spots : (k + 1) * spots] for k in range(cuts)], axis=1)
            for frame in range(frames)
        ],
        axis=0,
    )


class Exchange:
    def __init__(self, group, stage, landing, sems):
        self.group, self.stage, self.landing, self.sems = group, stage, landing, sems

    def copy(self, block, far):
        g = self.group
        other = g.other_frame(far)
        return remote(
            self.stage.at[block, other], self.landing.at[block, g.frame], self.sems, far - 1, block, other, "frames"
        )

    def push(self, block, values):
        frames = self.group.frames
        for frame, piece in enumerate(pack(values, frames)):
            self.stage[block, frame] = piece.astype(BF)
        self.landing[block, self.group.frame] = self.stage[block, self.group.frame]
        for far in range(1, frames):
            self.copy(block, far).start()

    def arrive(self, block):
        for far in range(1, self.group.frames):
            self.copy(block, far).wait_recv()

    def sent(self, block):
        for far in range(1, self.group.frames):
            self.copy(block, far).wait_send()

    @staticmethod
    def scratch(shape):
        return [pltpu.VMEM(shape, BF), pltpu.SemaphoreType.DMA((2, shape[1] - 1, shape[0]))]


class Reduce:
    def __init__(self, group_size, slack, load, group, source, result, stage, landing, sems, own, own_sems):
        self.group_size, self.slack, self.load = group_size, slack, load
        self.group, self.source, self.result = group, source, result
        self.stage, self.landing, self.sems = stage, landing, sems
        self.own, self.own_sems = own, own_sems
        self.chunks, self.pieces = result.shape[:2]
        self.levels = group.levels

    def half(self, level):
        return self.pieces >> (level + 1)

    def choice(self, chunk, level, normal):
        turned = self.group.c * (1 - (chunk + self.chunks - 3) // self.chunks)
        return normal[level] + turned * (normal[(level + 1) % self.levels] - normal[level])

    def bit(self, chunk, level):
        return self.choice(chunk, level, self.group.bits)

    def partner(self, chunk, level):
        return self.choice(chunk, level, self.group.partners)

    def offset(self, chunk, level):
        return sum((self.bit(chunk, k) * self.half(k) for k in range(level)), 0)

    def place(self, level):
        return pl.ds(self.pieces - (self.pieces >> level), self.half(level))

    def down(self, chunk, level):
        place = self.place(level)
        return remote(
            self.stage.at[chunk, place],
            self.landing.at[chunk, place],
            self.sems,
            level,
            chunk,
            self.partner(chunk, level),
            "frames",
        )

    def up(self, chunk, level):
        done = self.result.at[chunk, pl.ds(self.offset(chunk, level + 1), self.half(level))]
        source = self.own.at[chunk] if level == self.levels - 1 else done
        return remote(source, done, self.sems, self.levels + level, chunk, self.partner(chunk, level), "frames")

    def keep(self, chunk):
        mine = self.result.at[chunk, pl.ds(self.offset(chunk, self.levels), 1)]
        return pltpu.make_async_copy(self.own.at[chunk], mine, self.own_sems.at[chunk])

    def put(self, chunk, level):
        half = self.half(level)
        given = self.offset(chunk, level) + (1 - self.bit(chunk, level)) * half
        self.stage[chunk, self.place(level)] = self.source[chunk, pl.ds(given, half)].astype(BF)
        self.down(chunk, level).start()

    def add(self, chunk, level):
        self.down(chunk, level).wait_recv()
        kept = pl.ds(self.offset(chunk, level + 1), self.half(level))
        self.source[chunk, kept] = self.source[chunk, kept] + self.landing[chunk, self.place(level)].astype(F32)

    def advance(self, chunk, turn):
        levels = self.levels
        if turn == 0:
            if self.load is not None:
                self.load.wait(chunk)
            self.put(chunk, 0)
        elif turn < levels:
            self.add(chunk, turn - 1)
            self.put(chunk, turn)
        elif turn == levels:
            self.add(chunk, levels - 1)
            mine = pl.ds(self.offset(chunk, levels), 1)
            self.own[chunk] = self.source[chunk, mine].astype(BF)
            self.keep(chunk).start()
            self.up(chunk, levels - 1).start()
        else:
            if turn == levels + 1:
                self.keep(chunk).wait()
            self.up(chunk, 2 * levels - turn).wait_recv()
            self.up(chunk, 2 * levels - turn - 1).start()

    def tick(self, time):
        for turn in range(2 * self.levels):
            first = time - turn - (self.slack if turn else 0)

            @pl.when((first >= 0) & (first < self.chunks // self.group_size))
            def _():
                for k in range(self.group_size):
                    self.advance(first * self.group_size + k, turn)

    def last(self):
        return self.chunks // self.group_size + 2 * self.levels - 2 + self.slack

    def finish(self):
        def done(chunk, carry):
            if self.levels == 1:
                self.keep(chunk).wait()
            self.up(chunk, 0).wait_recv()
            for level in range(self.levels):
                self.down(chunk, level).wait_send()
                self.up(chunk, level).wait_send()
            return carry

        lax.fori_loop(0, self.chunks, done, 0)

    @staticmethod
    def scratch(shape):
        chunks, pieces, part, width = shape
        levels = pieces.bit_length() - 1
        return [
            pltpu.VMEM((chunks, pieces - 1, part, width), BF),
            pltpu.VMEM((chunks, pieces - 1, part, width), BF),
            pltpu.SemaphoreType.DMA((2, 2 * levels, chunks)),
            pltpu.VMEM((chunks, 1, part, width), BF),
            pltpu.SemaphoreType.DMA((chunks,)),
        ]


class SmallSum:
    def __init__(self, group, total, out, landing, sems):
        self.peers = group.everyone()
        self.total, self.out, self.landing, self.sems = total, out, landing, sems

    def copy(self, turn):
        axis, peer = self.peers[turn]
        return remote(self.out.at[turn], self.landing.at[turn], self.sems, 0, turn, peer, axis)

    def tick(self, time):
        for turn in range(len(self.peers) + 1):

            @pl.when(time == turn)
            def _():
                if turn > 0:
                    self.copy(turn - 1).wait_recv()
                    self.total[...] += self.landing[turn - 1]
                if turn < len(self.peers):
                    self.out[turn] = self.total[...]
                    self.copy(turn).start()

    def last(self):
        return len(self.peers)

    def finish(self):
        for turn in range(len(self.peers)):
            self.copy(turn).wait_send()

    @staticmethod
    def scratch(peers, shape):
        return [
            pltpu.VMEM((peers,) + shape, F32),
            pltpu.VMEM((peers,) + shape, F32),
            pltpu.SemaphoreType.DMA((2, 1, peers)),
        ]


class Bulk:
    def __init__(self, group, source, landing, sems, own_sem):
        self.group, self.source, self.landing, self.sems = group, source, landing, sems
        frame = group.frame
        self.own = pltpu.make_async_copy(source.at[frame], landing.at[frame], own_sem)

    def copy(self, far):
        other = self.group.other_frame(far)
        return remote(
            self.source.at[other], self.landing.at[self.group.frame], self.sems, 0, far - 1, other, "frames"
        )

    def start(self):
        self.own.start()
        for far in range(1, self.group.frames):
            self.copy(far).start()

    def finish(self):
        self.own.wait()
        for far in range(1, self.group.frames):
            self.copy(far).wait()

    @staticmethod
    def scratch(frames):
        return [pltpu.SemaphoreType.DMA((2, 1, frames - 1)), pltpu.SemaphoreType.DMA]


class Twice:
    def __init__(self, scatter, before):
        self.scatter, self.before = scatter, before

    def cross(self, pair):
        for k in range(2):
            self.scatter.cross(2 * pair + k + self.before)


class Move:
    def __init__(self, pairs, sems, shift=0):
        self.pairs, self.sems, self.shift = pairs, sems, shift

    def copies(self, block):
        return [
            pltpu.make_async_copy(
                src.at[block % src.shape[0]], dst.at[(block + self.shift) % dst.shape[0]], self.sems.at[k, block]
            )
            for k, (src, dst) in enumerate(self.pairs)
        ]

    def start(self, block):
        for copy in self.copies(block):
            copy.start()

    def wait(self, block):
        for copy in self.copies(block):
            copy.wait()


def pipeline(phases, steps=0, beside=None):
    def step(i, carry):
        for lag in (0, 1, 2, LAG):
            first = 0
            for blocks, gathers, scatters, compute, take in phases:
                block = i - lag - first
                first += blocks

                @pl.when((block >= 0) & (block < blocks))
                def _():
                    if lag == 0:
                        for gather in gathers:
                            gather.forward(block)
                    elif lag == 1:
                        for gather in gathers:
                            gather.arrive(block)
                        compute(block)
                    elif lag == 2:
                        for scatter, before in scatters:
                            scatter.cross(block + before)
                    elif take is not None:
                        take(block)

        if beside is not None:
            beside(i)
        return carry

    lax.fori_loop(0, max(sum(phase[0] for phase in phases) + LAG, steps), step, 0)
    for scatter in {id(scatter): scatter for phase in phases for scatter, _ in phase[2]}.values():
        if isinstance(scatter, Scatter):
            scatter.finish()


def coded_rows(codes_ref, block, actions):
    return (lax.broadcasted_iota(jnp.int32, (actions, 1), 0) == codes_ref[0, block]).astype(F32)


def space_stream(stream_ref, codes_ref, table_ref, block):
    hot = coded_rows(codes_ref, block, table_ref.shape[0])
    added = jnp.sum(hot * table_ref[...].astype(F32), axis=0, keepdims=True)
    return stream_ref[block].astype(F32) + added


def row_of(gain_ref):
    return gain_ref[...].astype(F32)[None]


def attention_block(whole_ref, w_qkv_ref, w_out_ref, qkv_ref, att_ref, seen_ref):
    _, part, width = whole_ref.shape
    normed = whole_ref[...].reshape(4 * part, width)
    for member in range(3):
        qkv_ref[member] = dot(normed, w_qkv_ref[member], (1, 0)).astype(BF)
    att_ref[...] = attend(qkv_ref[0], qkv_ref[1], qkv_ref[2], seen_ref)
    return dot(att_ref[...], w_out_ref[...], (1, 0))


def each_block(blocks, work):
    def one(block, carry):
        work(block)
        return carry

    lax.fori_loop(0, blocks, one, 0)


def call(kernel, name, collective_id, operands, outs, scratch, flops):
    def specs(items):
        return [pl.BlockSpec(memory_space=space) for _, space in items]

    return pl.pallas_call(
        kernel,
        name=name,
        out_shape=[shape for shape, _ in outs],
        in_specs=specs(operands),
        out_specs=specs(outs),
        scratch_shapes=scratch,
        compiler_params=pltpu.CompilerParams(
            collective_id=collective_id, has_side_effects=True, vmem_limit_bytes=LIMIT
        ),
        cost_estimate=pl.CostEstimate(flops=flops, bytes_accessed=16 << 20, transcendentals=0),
    )(*(array for array, _ in operands))


def inside(*items):
    return [(item, pltpu.VMEM) for item in items]


def outside(*items):
    return [(item, pl.ANY) for item in items]


def scalars(item):
    return [(item, pltpu.SMEM)]


def held_like(shapes):
    return [pltpu.VMEM(shape.shape, shape.dtype) for shape in shapes] + [
        pltpu.SemaphoreType.DMA((len(shapes), shapes[0].shape[0]))
    ]


def saved_shapes(blocks, part, width, inner):
    return [
        jax.ShapeDtypeStruct((blocks, 4, part, width), BF),
        jax.ShapeDtypeStruct((blocks, 3, 4 * part, inner), BF),
        jax.ShapeDtypeStruct((blocks, 4 * part, inner), BF),
    ]


def backward_kernel(
    frames,
    grad_ref,
    stream_ref,
    tokens_ref,
    codes_ref,
    table_ref,
    gain_sp_ref,
    gain_tm_ref,
    gain_ff_out,
    w_qkv_sp_ref,
    w_out_sp_ref,
    w_qkv_tm_ref,
    w_out_tm_ref,
    *refs,
):
    time_saved, space_saved, refs = refs[:3], refs[3:6], refs[6:]
    rest_in, mixed_ref, out_ref, space_total, time_total, rest_total, small_ref, mixed_out_ref, *refs = refs
    small_clips, seen_ref, mixed_sems, own_sem, stage, stage_sems, landing, *refs = refs
    slots, refs = refs[:3], refs[3:]
    time_load_sems, space_load_sems, rest_load_sems, w_sum, shared_sum, *refs = refs
    grad_whole_ref, packed_ref, time_sems, space_sems, *refs = refs
    whole_ref, qkv_ref, att_ref = slots
    blocks, _, part, width = grad_whole_ref.shape
    rows = 4 * part
    group = Group(frames, True)
    group.meet()
    time_gather = Gather(group, grad_whole_ref, time_sems)
    space_gather = Gather(group, grad_whole_ref, space_sems)
    scatter = Scatter(group, *refs[:6])
    rest_load = Move([(rest_in, shared_sum)], rest_load_sems)
    rest_reduce = Reduce(2, 1, rest_load, group, shared_sum, rest_total, *refs[6:11])
    time_reduce = Reduce(2, 1, None, group, w_sum, time_total, *refs[11:16])
    space_reduce = Reduce(1, 0, None, group, shared_sum, space_total, *refs[6:8], *refs[16:19])
    small = SmallSum(group, small_ref, *refs[19:])
    exchange = Exchange(group, stage, landing, stage_sems)
    mixed_bulk = Bulk(group, mixed_ref, mixed_out_ref, mixed_sems, own_sem)
    time_load = Move(list(zip(time_saved, slots)), time_load_sems)
    space_load = Move(list(zip(space_saved, slots)), space_load_sems, blocks)
    ahead = whole_ref.shape[0] - 1

    def gather_grad(gather, block, grad):
        grad_whole_ref[block, group.me] = grad.astype(BF)
        gather.start(block)

    each_block(blocks, lambda block: gather_grad(time_gather, block, grad_ref[block]))
    each_block(ahead, time_load.start)
    each_block(CHUNKS, rest_load.start)
    mixed_bulk.start()
    w_sum[...] = jnp.zeros_like(w_sum)
    seen_ref[...] = visible(rows, frames, 1).astype(F32)
    small_ref[...] = jnp.zeros_like(small_ref)
    small_ref[10:11, :] = gain_ff_out[...]

    def back(block, at, w_qkv_ref):
        scatter.free(at)
        scatter.send(at, sum(dot(packed_ref[block, member], w_qkv_ref[member], (1, 1)) for member in range(3)))

    def attention(block, slot, w_out_ref, sums, seen):
        grad_y = grad_whole_ref[block].reshape(rows, width)
        grad_att = dot(grad_y, w_out_ref[...], (1, 1)).astype(BF)
        grads = attend_back(qkv_ref[slot, 0], qkv_ref[slot, 1], qkv_ref[slot, 2], grad_att, seen)
        for member in range(3):
            packed_ref[block, member] = grads[member]
        piece = sums.shape[1:]
        normed = whole_ref[slot].reshape(rows, width)
        quarter = width // 4
        for member in range(4):
            small = packed_ref[block, member] if member < 3 else att_ref[slot]
            wide = normed if member < 3 else grad_y
            grad_w = dot(small, wide, (0, 0))
            cuts = [grad_w[:, k * quarter : (k + 1) * quarter] for k in range(4)]
            for k in range(2):
                sums[2 * member + k] += jnp.concatenate(cuts[2 * k : 2 * k + 2], axis=0).reshape(piece)

    def time_compute(block):
        time_load.wait(block)

        @pl.when(block + ahead < blocks)
        def _():
            time_load.start(block + ahead)

        @pl.when(block + ahead >= blocks)
        def _():
            space_load.start(block + ahead - blocks)

        attention(block, block % (ahead + 1), w_out_tm_ref, w_sum, seen_ref)
        time_gather.sent(block)
        back(block, block, w_qkv_tm_ref)

    def time_take(block):
        stream = unpack(stream_ref[block], width)
        grad_part, grad_gain = norm_backward(scatter.take(block), stream, row_of(gain_tm_ref))
        exchange.push(block, grad_ref[block] + grad_part)
        small_ref[9:10, :] += grad_gain

    def space_compute(block):
        space_load.wait(block)

        @pl.when(block + ahead < blocks)
        def _():
            space_load.start(block + ahead)

        attention(block, (block + blocks) % (ahead + 1), w_out_sp_ref, shared_sum, None)

    def space_back(pair):
        for k in range(2):
            back(2 * pair + k, 2 * pair + k + blocks, w_qkv_sp_ref)

    def space_take(pair):
        for k in range(2):
            block = 2 * pair + k
            stream = space_stream(tokens_ref, codes_ref, table_ref, block)
            grad_part, grad_gain = norm_backward(scatter.take(block + blocks), stream, row_of(gain_sp_ref))
            grad_stream = unpack(landing[block], width) + grad_part
            out_ref[block] = grad_stream
            small_ref[8:9, :] += grad_gain
            small_clips[pl.ds(block, 1)] = jnp.sum(grad_stream, axis=0, keepdims=True)[None]

    launch_lag = LAG + 2
    space_first = blocks + GAP
    space_done = space_first + blocks
    taken = space_done + blocks // 2 + LAG - 1

    def beside(i):
        block = i - launch_lag

        @pl.when((block >= 0) & (block < blocks))
        def _():
            exchange.arrive(block)
            gather_grad(space_gather, block, unpack(landing[block], width))

        rest_reduce.tick(i)
        time_reduce.tick(i - blocks)

        @pl.when(i == space_first)
        def _():
            shared_sum[...] = jnp.zeros_like(shared_sum)

        @pl.when(i == space_done - 1)
        def _():
            rest_reduce.finish()

        space_reduce.tick(i - space_done)

        @pl.when(i == taken)
        def _():
            for clip in range(blocks):
                small_ref[0:8, :] += coded_rows(codes_ref, clip, 8) * small_clips[clip]

        small.tick(i - taken)

    pipeline(
        [
            (blocks, [time_gather], [(scatter, 0)], time_compute, time_take),
            (GAP, [], [], lambda block: None, None),
            (blocks, [space_gather], [], space_compute, None),
            (blocks // 2, [], [(Twice(scatter, blocks), 0)], space_back, space_take),
        ],
        max(space_done + space_reduce.last() + 1, taken + small.last() + 1),
        beside,
    )
    each_block(blocks, space_gather.sent)
    each_block(blocks, exchange.sent)
    for moved in (time_reduce, space_reduce, small, mixed_bulk):
        moved.finish()


def backward(frames, grad, stream, tokens, codes, table, gains, weights, kept, rest_sum, mixed):
    blocks, part, width = tokens.shape
    inner = weights[1].shape[0]
    rows = 4 * part
    packed = packed_shape(blocks, frames, part, width)
    sums = (CHUNKS, frames, 2 * inner // frames, width // 4)
    small = (16, width)
    peers = 2 + frames.bit_length() - 1
    reduce = Reduce.scratch(sums)
    return call(
        functools.partial(backward_kernel, frames),
        "backward",
        2,
        inside(grad, stream, tokens)
        + scalars(codes)
        + inside(table, *gains, *weights)
        + outside(*kept, rest_sum, mixed),
        inside(jax.ShapeDtypeStruct(tokens.shape, F32))
        + outside(*[jax.ShapeDtypeStruct(sums, BF)] * 3)
        + inside(jax.ShapeDtypeStruct(small, F32))
        + outside(jax.ShapeDtypeStruct(mixed.shape, BF)),
        [pltpu.VMEM((blocks, 1, width), F32), pltpu.VMEM((rows, rows), F32)]
        + Bulk.scratch(frames)
        + Exchange.scratch(packed)
        + [pltpu.VMEM(packed, BF)]
        + [pltpu.VMEM((3,) + each.shape[1:], BF) for each in kept[:3]]
        + [pltpu.SemaphoreType.DMA((3, blocks))] * 2
        + [pltpu.SemaphoreType.DMA((1, CHUNKS)), pltpu.VMEM(sums, F32), pltpu.VMEM(sums, F32)]
        + [pltpu.VMEM((blocks, 4, part, width), BF), pltpu.VMEM((blocks, 3, rows, inner), BF)]
        + [Gather.scratch(blocks)] * 2
        + Scatter.scratch(2 * blocks, blocks, part, width)
        + reduce
        + reduce
        + reduce[2:]
        + SmallSum.scratch(peers, small),
        1 << 30,
    )


def gelu_parts(hidden):
    slope = 0.7978845608028654
    square = hidden * hidden
    bent = jnp.tanh(slope * hidden * (1.0 + 0.044715 * square))
    half = 0.5 * (1.0 + bent)
    grad = half + 0.5 * hidden * (1.0 - bent * bent) * (slope * (1.0 + 3 * 0.044715 * square))
    return hidden * half, grad


def forward_kernel(
    frames,
    tokens_ref,
    codes_ref,
    table_ref,
    cot_in,
    gain_sp_ref,
    gain_tm_ref,
    gain_ff_ref,
    w_qkv_sp_ref,
    w_out_sp_ref,
    w_qkv_tm_ref,
    w_out_tm_ref,
    w_up_in,
    w_down_in,
    stream_ref,
    mixed_ref,
    grad_ref,
    gain_out_ref,
    total_ref,
    sum_out,
    *refs,
):
    space_saved, time_saved, refs = refs[:3], refs[3:6], refs[6:]
    w_sum, rest_sum, sum_sems, w_up_ref, w_down_ref, w_sems, *refs = refs
    whole_ref, qkv_ref, att_ref, space_sems, time_sems, seen_ref, stage, stage_sems, *refs = refs
    cot_ref, bulk_sems, own_sem, cot_whole_ref, sp_sems, tm_sems, ffn_sems, cot_sems, *refs = refs
    blocks, _, part, width = whole_ref.shape
    rows = 4 * part
    half = w_up_ref.shape[2] // 2
    group = Group(frames, True)
    group.meet()
    space_gather = Gather(group, whole_ref, sp_sems)
    time_gather = Gather(group, whole_ref, tm_sems)
    ffn_gather = Gather(group, whole_ref, ffn_sems)
    cot_gather = Gather(group, cot_whole_ref, cot_sems)
    scatter = Scatter(group, *refs[:6])
    grad_scatter = Scatter(group, *refs[6:12])
    reduce = Reduce(2, 1, None, group, w_sum, total_ref, *refs[12:])
    exchange = Exchange(group, stage, stream_ref, stage_sems)
    cot_bulk = Bulk(group, cot_in, cot_ref, bulk_sems, own_sem)
    w_load = Move([(w_up_in, w_up_ref), (w_down_in, w_down_ref)], w_sems)
    sum_save = Move([(rest_sum, sum_out)], sum_sems)

    def gather_normed(gather, block, stream, gain_ref):
        unit, _ = norm_parts(stream)
        whole_ref[block, group.me] = (unit * row_of(gain_ref)).astype(BF)
        gather.start(block)

    def begin(block):
        gather_normed(space_gather, block, space_stream(tokens_ref, codes_ref, table_ref, block), gain_sp_ref)

    each_block(blocks, begin)
    cot_bulk.start()
    w_load.start(0)
    seen_ref[...] = visible(rows, frames).astype(F32)
    w_sum[...] = jnp.zeros_like(w_sum)
    rest_sum[...] = jnp.zeros_like(rest_sum)
    gain_out_ref[...] = jnp.zeros_like(gain_out_ref)

    def attention(block, gather, saved, sems, w_qkv_ref, w_out_ref, seen, at):
        whole_save = Move([(whole_ref, saved[0])], sems.at[0:1])
        save = Move([(qkv_ref, saved[1]), (att_ref, saved[2])], sems.at[1:3])
        whole_save.start(block)

        @pl.when(block >= 2)
        def _():
            save.wait(block - 2)

        slot = block % 2
        result = attention_block(whole_ref.at[block], w_qkv_ref, w_out_ref, qkv_ref.at[slot], att_ref.at[slot], seen)
        save.start(block)
        gather.sent(block)
        whole_save.wait(block)
        scatter.free(at)
        scatter.send(at, result)

        @pl.when(block == blocks - 1)
        def _():
            save.wait(blocks - 2)
            save.wait(blocks - 1)

    def space_compute(block):
        attention(block, space_gather, space_saved, space_sems, w_qkv_sp_ref, w_out_sp_ref, None, block)

    def time_compute(block):
        at = block + blocks
        attention(block, time_gather, time_saved, time_sems, w_qkv_tm_ref, w_out_tm_ref, seen_ref, at)

    def space_take(block):
        exchange.push(block, space_stream(tokens_ref, codes_ref, table_ref, block) + scatter.take(block))

    def time_take(block):
        stream = unpack(stream_ref[block], width) + scatter.take(block + blocks)
        grad_ref[block] = stream
        gather_normed(ffn_gather, block, stream, gain_ff_ref)
        cot_whole_ref[block, group.me] = unpack(cot_ref[:, block], width).astype(BF)
        cot_gather.start(block)

    def ffn_compute(block, second):
        sums = rest_sum if second else w_sum
        hidden = pl.ds(half if second else 0, half)
        normed = whole_ref[block].reshape(rows, width)
        grad_y = cot_whole_ref[block].reshape(rows, width)
        w_up = w_up_ref[0, :, hidden]
        w_down = w_down_ref[0, hidden, :]
        activated, slope = gelu_parts(dot(normed, w_up, (1, 0)))
        activated = activated.astype(BF)
        grad_pre = (dot(grad_y, w_down, (1, 1)) * slope).astype(BF)
        if not second:
            scatter.free(block + 2 * blocks)
        for each, at, values in (
            (scatter, block + 2 * blocks, dot(activated, w_down, (1, 0))),
            (grad_scatter, block, dot(grad_pre, w_up, (1, 1))),
        ):
            if second:
                each.send(at, values, True)
            else:
                each.put(at, values)
        for first, small, wide in ((0, grad_pre, normed), (4, activated, grad_y)):
            grad_w = dot(small, wide, (0, 0))
            for k in range(4):
                cut = grad_w[:, k * (width // 4) : (k + 1) * (width // 4)]
                sums[first + k] += cut.reshape(sums.shape[1:])

    def take(block):
        stream = grad_ref[block]
        for frame, piece in enumerate(pack(stream + scatter.take(block + 2 * blocks), frames)):
            mixed_ref[frame, block] = piece.astype(BF)
        grad_part, grad_gain = norm_backward(grad_scatter.take(block), stream, row_of(gain_ff_ref))
        grad_ref[block] = cot_whole_ref[block, group.me].astype(F32) + grad_part
        gain_out_ref[...] += grad_gain

    launch_lag = LAG + 2
    ffn_first = 2 * blocks + GAP

    def beside(i):
        block = i - launch_lag

        @pl.when((block >= 0) & (block < blocks))
        def _():
            exchange.arrive(block)
            gather_normed(time_gather, block, unpack(stream_ref[block], width), gain_tm_ref)

        @pl.when(i == blocks + GAP)
        def _():
            cot_bulk.finish()

        @pl.when(i == ffn_first)
        def _():
            w_load.wait(0)

        reduce.tick(i - ffn_first - blocks)

        @pl.when(i == ffn_first + 2 * blocks)
        def _():
            each_block(CHUNKS, sum_save.start)

    pipeline(
        [
            (blocks, [space_gather], [(scatter, 0)], space_compute, space_take),
            (GAP, [], [], lambda block: None, None),
            (blocks, [time_gather], [(scatter, blocks)], time_compute, time_take),
            (blocks, [ffn_gather, cot_gather], [], lambda block: ffn_compute(block, False), None),
            (blocks, [], [(scatter, 2 * blocks), (grad_scatter, 0)], lambda block: ffn_compute(block, True), take),
        ],
        ffn_first + blocks + reduce.last() + 1,
        beside,
    )
    each_block(blocks, ffn_gather.sent)
    each_block(blocks, cot_gather.sent)
    each_block(blocks, exchange.sent)
    reduce.finish()
    each_block(CHUNKS, sum_save.wait)


def forward(frames, tokens, codes, table, cot, gains, w_qkv_sp, w_out_sp, w_qkv_tm, w_out_tm, w_up, w_down):
    blocks, part, width = tokens.shape
    inner = w_out_sp.shape[0]
    packed = packed_shape(blocks, frames, part, width)
    whole = pltpu.VMEM((blocks, 4, part, width), BF)
    saved = saved_shapes(blocks, part, width, inner)
    sums = jax.ShapeDtypeStruct((CHUNKS, frames, w_up.shape[1] // (2 * frames), width // 4), F32)
    weights = [w_up[None], w_down[None]]
    return call(
        functools.partial(forward_kernel, frames),
        "forward_and_ffn",
        1,
        inside(tokens)
        + scalars(codes)
        + inside(table)
        + outside(cot)
        + inside(*gains, w_qkv_sp, w_out_sp, w_qkv_tm, w_out_tm)
        + outside(*weights),
        inside(
            jax.ShapeDtypeStruct(packed, BF),
            jax.ShapeDtypeStruct(cot.shape, BF),
            jax.ShapeDtypeStruct((blocks, part, width), F32),
            jax.ShapeDtypeStruct((1, width), F32),
        )
        + outside(jax.ShapeDtypeStruct(sums.shape, BF), sums, *saved, *saved),
        [pltpu.VMEM(sums.shape, F32), pltpu.VMEM(sums.shape, F32), pltpu.SemaphoreType.DMA((1, CHUNKS))]
        + held_like(weights)
        + [
            whole,
            pltpu.VMEM((2,) + saved[1].shape[1:], BF),
            pltpu.VMEM((2,) + saved[2].shape[1:], BF),
            pltpu.SemaphoreType.DMA((3, blocks)),
            pltpu.SemaphoreType.DMA((3, blocks)),
            pltpu.VMEM((4 * part, 4 * part), F32),
        ]
        + Exchange.scratch(packed)
        + [pltpu.VMEM(cot.shape, BF)]
        + Bulk.scratch(frames)
        + [whole]
        + [Gather.scratch(blocks)] * 4
        + Scatter.scratch(3 * blocks, blocks, part, width)
        + Scatter.scratch(blocks, blocks, part, width)
        + Reduce.scratch(sums.shape),
        (16 * inner + 12 * w_up.shape[1]) * blocks * 4 * part * width,
    )


def widen_kernel(space_ref, time_ref, first_ref, second_ref, mixed_ref, tokens_ref, small_ref, *outs):
    step = pl.program_id(0)
    mixed_out, tokens_out, table_out, *gain_outs = outs[:6]
    for sums_ref, qkv_out, w_out_out in ((space_ref, *outs[6:8]), (time_ref, *outs[8:10])):
        quarter = sums_ref.shape[3]

        @pl.when(step < 6)
        def _():
            for k in range(2):
                qkv_out[0, k * quarter : (k + 1) * quarter] = sums_ref[0, k].T.astype(F32)

        @pl.when(step >= 6)
        def _():
            for k in range(2):
                w_out_out[:, k * quarter : (k + 1) * quarter] = sums_ref[0, k].astype(F32)

    up_out, down_out = outs[10:]
    hidden = first_ref.shape[1]

    @pl.when(step < 4)
    def _():
        for k, ffn_ref in enumerate((first_ref, second_ref)):
            up_out[:, k * hidden : (k + 1) * hidden] = ffn_ref[0].T.astype(F32)

    @pl.when(step >= 4)
    def _():
        for k, ffn_ref in enumerate((first_ref, second_ref)):
            down_out[k * hidden : (k + 1) * hidden] = ffn_ref[0].astype(F32)

    for block in range(mixed_ref.shape[1]):
        mixed_out[block] = unpack(mixed_ref[:, block], mixed_out.shape[2]).astype(BF)
    tokens_out[...] = tokens_ref[...]

    @pl.when(step == 0)
    def _():
        table_out[...] = small_ref[0:8, :]
        for k, gain_out in enumerate(gain_outs):
            gain_out[...] = small_ref[8 + k : 9 + k, :]


def widen(frames, space_sums, time_sums, first_sums, second_sums, mixed, tokens, small, inner):
    blocks, part, width = tokens.shape
    quarter = width // 4
    hidden = 2 * first_sums.shape[1] * first_sums.shape[2]
    whole = lambda i: (0, 0)
    some = pl.BlockSpec((blocks // CHUNKS, part, width), lambda i: (i, 0, 0))
    turned = [
        (
            jax.ShapeDtypeStruct((3, width, inner), F32),
            pl.BlockSpec((1, 2 * quarter, inner), lambda i: (jnp.minimum(i, 5) // 2, jnp.minimum(i, 5) % 2, 0)),
        ),
        (
            jax.ShapeDtypeStruct((inner, width), F32),
            pl.BlockSpec((inner, 2 * quarter), lambda i: (0, jnp.maximum(i - 6, 0))),
        ),
    ]
    outs = [(jax.ShapeDtypeStruct(tokens.shape, BF), some), (jax.ShapeDtypeStruct(tokens.shape, F32), some)]
    outs += [(jax.ShapeDtypeStruct((8, width), F32), pl.BlockSpec((8, width), whole))]
    outs += [(jax.ShapeDtypeStruct((1, width), F32), pl.BlockSpec((1, width), whole))] * 3 + turned + turned
    outs += [
        (
            jax.ShapeDtypeStruct((width, hidden), F32),
            pl.BlockSpec((quarter, hidden), lambda i: (jnp.minimum(i, 3), 0)),
        ),
        (
            jax.ShapeDtypeStruct((hidden, width), F32),
            pl.BlockSpec((hidden, quarter), lambda i: (0, jnp.maximum(i - 4, 0))),
        ),
    ]
    chunk = pl.BlockSpec((1, 2, inner, quarter), lambda i: (i, 0, 0, 0))
    ffn_chunk = pl.BlockSpec((1, hidden // 2, quarter), lambda i: (i, 0, 0))
    return pl.pallas_call(
        widen_kernel,
        name="widen",
        grid=(CHUNKS,),
        out_shape=[shape for shape, _ in outs],
        in_specs=[
            chunk,
            chunk,
            ffn_chunk,
            ffn_chunk,
            pl.BlockSpec((frames, blocks // CHUNKS) + mixed.shape[2:], lambda i: (0, i, 0, 0)),
            some,
            pl.BlockSpec(small.shape, whole),
        ],
        out_specs=[spec for _, spec in outs],
        compiler_params=pltpu.CompilerParams(vmem_limit_bytes=LIMIT),
    )(
        space_sums.reshape(CHUNKS, 2, inner, quarter),
        time_sums.reshape(CHUNKS, 2, inner, quarter),
        first_sums.reshape(CHUNKS, hidden // 2, quarter),
        second_sums.reshape(CHUNKS, hidden // 2, quarter),
        mixed,
        tokens,
        small,
    )


def pack_rows(values, frames):
    blocks, part, width = values.shape
    shape = packed_shape(blocks, frames, part, width)
    cut = values.reshape(blocks, frames, part // frames, width // shape[-1], shape[-1])
    return cut.transpose(1, 0, 3, 2, 4).reshape((frames, blocks) + shape[2:])


def body(
    frames,
    tokens,
    codes,
    table,
    gain_space,
    gain_time,
    gain_ffn,
    w_qkv_space,
    w_out_space,
    w_qkv_time,
    w_out_time,
    w_up,
    w_down,
    cotangent,
):
    gain_sp, gain_tm, gain_ff = gain_space, gain_time, gain_ffn
    w_qkv_sp = w_qkv_space.swapaxes(0, 1)
    w_qkv_tm = w_qkv_time.swapaxes(0, 1)
    _, blocks, part, width = tokens.shape

    gains = gain_sp, gain_tm, gain_ff
    weights = w_qkv_sp, w_out_space, w_qkv_tm, w_out_time, w_up, w_down
    stream_one, mixed, grad_two, grad_gain_ff, first_totals, ffn_sums, *kept = forward(
        frames, tokens[0], codes, table, pack_rows(cotangent[0], frames), gains, *weights
    )
    grad_zero, space_totals, time_totals, ffn_totals, small, mixed = backward(
        frames,
        grad_two,
        stream_one,
        tokens[0],
        codes,
        table,
        (gain_sp, gain_tm, grad_gain_ff),
        weights[:4],
        kept[3:] + kept[:3],
        ffn_sums,
        mixed,
    )
    mixed, grad_zero, grad_tab, gain_sp, gain_tm, gain_ff, *grads = widen(
        frames, space_totals, time_totals, first_totals, ffn_totals, mixed, grad_zero, small, w_out_space.shape[0]
    )
    return (
        mixed[None],
        grad_zero[None],
        grad_tab,
        gain_sp[0],
        gain_tm[0],
        gain_ff[0],
        grads[0].swapaxes(0, 1),
        grads[1],
        grads[2].swapaxes(0, 1),
        grads[3],
        *grads[4:],
    )


def solution(mesh):
    rows = P("frames", None, "tensor", None)
    return jax.shard_map(
        functools.partial(body, mesh.shape["frames"]),
        mesh=mesh,
        in_specs=(
            rows,
            P("frames", None),
            P(),
            P(),
            P(),
            P(),
            P(None, None, "tensor"),
            P("tensor", None),
            P(None, None, "tensor"),
            P("tensor", None),
            P(None, "tensor"),
            P("tensor", None),
            rows,
        ),
        out_specs=(
            rows,
            rows,
            P(),
            P(),
            P(),
            P(),
            P(None, None, "tensor"),
            P("tensor", None),
            P(None, None, "tensor"),
            P("tensor", None),
            P(None, "tensor"),
            P("tensor", None),
        ),
        check_vma=False,
    )
```

```python
import functools

import jax
import jax.numpy as jnp
from jax import lax
from jax.experimental import pallas as pl
from jax.experimental.pallas import tpu as pltpu
from jax.sharding import PartitionSpec as P

HD = 64
EPS = 1e-06
BF = jnp.bfloat16
F32 = jnp.float32
MESH = pl.DeviceIdType.MESH
LIMIT = 63 * 1024 * 1024
LAG = 4
GAP = 1
CHUNKS = 8


def dot(left, right, contract):
    return lax.dot_general(left, right, ((contract[:1], contract[1:]), ((), ())), preferred_element_type=F32)


def norm_parts(values):
    factor = lax.rsqrt(jnp.mean(values * values, axis=-1, keepdims=True) + EPS)
    return values * factor, factor


def norm_backward(grad_normed, stream, gain_vec):
    unit, factor = norm_parts(stream)
    scaled = grad_normed * gain_vec
    grad_stream = (scaled - unit * jnp.mean(scaled * unit, axis=-1, keepdims=True)) * factor
    return grad_stream, jnp.sum(grad_normed * unit, axis=0, keepdims=True)


def head_mask(rows, width, head):
    lane = lax.broadcasted_iota(jnp.int32, (rows, width), 1)
    return (lane >= head * HD) & (lane < (head + 1) * HD)


def visible(rows, frames, query_dim=0):
    part = rows // 4
    spots = part // frames
    row = lax.broadcasted_iota(jnp.int32, (rows, rows), query_dim)
    col = lax.broadcasted_iota(jnp.int32, (rows, rows), 1 - query_dim)
    same_part = row // part == col // part
    same_spot = row % spots == col % spots
    earlier = (col % part) // spots <= (row % part) // spots
    return same_part & same_spot & earlier


def block_probs(queries, keys_in, seen):
    scores = dot(queries, keys_in, (1, 1))
    if seen is not None:
        scores = jnp.where(seen[...] > 0, scores, -1e30)
    raised = jnp.exp(scores - jnp.max(scores, axis=-1, keepdims=True))
    return raised * (1.0 / jnp.sum(raised, axis=-1, keepdims=True))


def attend(queries, keys_in, values, seen):
    rows, width = queries.shape
    total = jnp.zeros((rows, width), F32)
    queries = queries * BF(HD ** (-0.5))
    for head in range(width // HD):
        mine = head_mask(rows, width, head)
        probs = block_probs(jnp.where(mine, queries, 0), keys_in, seen)
        total = total + dot(probs.astype(BF), jnp.where(mine, values, 0), (1, 0))
    return total.astype(BF)


def attend_back(queries, keys_in, values, grad_att, seen):
    rows, width = queries.shape
    zero = jnp.zeros((rows, width), F32)
    grad_q, grad_k, grad_v = zero, zero, zero
    scale = BF(HD ** (-0.5))
    queries = queries * scale
    scaled_keys = keys_in * scale
    for head in range(width // HD):
        mine = head_mask(rows, width, head)
        my_queries = jnp.where(mine, queries, 0)
        my_grad = jnp.where(mine, grad_att, 0)
        scores = dot(keys_in, my_queries, (1, 1))
        if seen is not None:
            scores = jnp.where(seen[...] > 0, scores, -1e30)
        raised = jnp.exp(scores - jnp.max(scores, axis=0, keepdims=True))
        probs = raised * (1.0 / jnp.sum(raised, axis=0, keepdims=True))
        grad_probs = dot(values, my_grad, (1, 1))
        row_dot = jnp.sum(grad_probs * probs, axis=0, keepdims=True)
        grad_scores = (probs * (grad_probs - row_dot)).astype(BF)
        grad_q = grad_q + dot(grad_scores, jnp.where(mine, scaled_keys, 0), (0, 0))
        grad_k = grad_k + dot(grad_scores, my_queries, (1, 0))
        grad_v = grad_v + dot(probs.astype(BF), my_grad, (1, 0))
    return grad_q.astype(BF), grad_k.astype(BF), grad_v.astype(BF)


class Group:
    def __init__(self, frames=1, all_frames=False):
        me = lax.axis_index("tensor")
        self.x, self.c = me // 2, me % 2
        self.me = me
        self.chip_peer = 2 * (1 - self.x) + self.c
        self.core_peer = 2 * self.x + 1 - self.c
        self.levels = frames.bit_length() - 1
        self.bits, self.partners = [], []
        self.frames, self.all_frames = frames, all_frames
        self.frame = frame = lax.axis_index("frames")
        for level in range(self.levels):
            bit = (frame // 2**level) % 2
            self.bits.append(bit)
            self.partners.append(frame + (1 - 2 * bit) * 2**level)

    def everyone(self):
        return [("tensor", self.chip_peer), ("tensor", self.core_peer)] + [
            ("frames", partner) for partner in self.partners
        ]

    def other_frame(self, distance):
        return (self.frame + distance) % self.frames

    def meet(self):
        barrier = pltpu.get_barrier_semaphore()
        peers = self.everyone()
        if self.all_frames:
            peers = peers[:2] + [("frames", self.other_frame(far)) for far in range(1, self.frames)]
        for axis, peer in peers:
            pl.semaphore_signal(barrier, inc=1, device_id={axis: peer}, device_id_type=MESH)
        pl.semaphore_wait(barrier, len(peers))


def remote(src, dst, sems, kind, block, peer, axis="tensor"):
    return pltpu.make_async_remote_copy(
        src_ref=src,
        dst_ref=dst,
        send_sem=sems.at[0, kind, block],
        recv_sem=sems.at[1, kind, block],
        device_id={axis: peer},
        device_id_type=MESH,
    )


class Gather:
    def __init__(self, group, whole, sems):
        self.group, self.whole, self.sems = group, whole, sems

    def copy(self, kind, block):
        g = self.group
        quarter = self.whole.at[block, g.chip_peer if kind == 2 else g.me]
        return remote(quarter, quarter, self.sems, kind, block, g.chip_peer if kind == 0 else g.core_peer)

    def start(self, block):
        self.copy(0, block).start()
        self.copy(1, block).start()

    def forward(self, block):
        self.copy(0, block).wait_recv()
        self.copy(2, block).start()

    def arrive(self, block):
        self.copy(1, block).wait_recv()
        self.copy(2, block).wait_recv()

    def sent(self, block):
        for kind in range(3):
            self.copy(kind, block).wait_send()

    @staticmethod
    def scratch(blocks):
        return pltpu.SemaphoreType.DMA((2, 3, blocks))


class Scatter:
    def __init__(self, group, kept, near_out, near_in, far_out, far_in, sems):
        self.group, self.kept, self.sems = group, kept, sems
        self.near_out, self.near_in, self.far_out, self.far_in = near_out, near_in, far_out, far_in
        self.slots, self.blocks = near_out.shape[0], sems.shape[2]

    def near(self, block):
        slot = block % self.slots
        return remote(self.near_out.at[slot], self.near_in.at[slot], self.sems, 0, block, self.group.core_peer)

    def far(self, block):
        slot = block % self.slots
        return remote(self.far_out.at[slot], self.far_in.at[slot], self.sems, 1, block, self.group.chip_peer)

    def free(self, block):
        if self.blocks > self.slots:

            @pl.when(block >= self.slots)
            def _():
                self.near(block - self.slots).wait_send()
                self.far(block - self.slots).wait_send()

    def put(self, block, values, more=False):
        slot = block % self.slots
        for x in range(2):
            first, second = (values[(2 * x + c) * self.part : (2 * x + c + 1) * self.part] for c in range(2))
            own = jnp.where(self.group.c == 0, first, second)
            given = jnp.where(self.group.c == 0, second, first)
            if more:
                own = own + self.kept[slot, x]
                given = given + self.near_out[slot, x].astype(F32)
            self.kept[slot, x] = own
            self.near_out[slot, x] = given.astype(BF)

    def send(self, block, values, more=False):
        self.put(block, values, more)
        self.near(block).start()

    @property
    def part(self):
        return self.kept.shape[2]

    def cross(self, block):
        x, slot = 1 - self.group.x, block % self.slots
        self.near(block).wait_recv()
        self.far_out[slot] = (self.kept[slot, x] + self.near_in[slot, x].astype(F32)).astype(BF)
        self.far(block).start()

    def take(self, block):
        x, slot = self.group.x, block % self.slots
        self.far(block).wait_recv()
        return self.kept[slot, x] + self.near_in[slot, x].astype(F32) + self.far_in[slot].astype(F32)

    def finish(self):
        def sent(block, carry):
            self.near(block).wait_send()
            self.far(block).wait_send()
            return carry

        lax.fori_loop(self.blocks - self.slots, self.blocks, sent, 0)

    @staticmethod
    def scratch(blocks, slots, part, width):
        return [
            pltpu.VMEM((slots, 2, part, width), F32),
            pltpu.VMEM((slots, 2, part, width), BF),
            pltpu.VMEM((slots, 2, part, width), BF),
            pltpu.VMEM((slots, part, width), BF),
            pltpu.VMEM((slots, part, width), BF),
            pltpu.SemaphoreType.DMA((2, 2, blocks)),
        ]


def packed_shape(blocks, frames, part, width):
    spots = part // frames
    cuts = max(1, 16 // spots)
    return (blocks, frames, cuts * spots, width // cuts)


def pack(values, frames):
    rows, width = values.shape
    spots = rows // frames
    cuts = max(1, 16 // spots)
    wide = width // cuts
    return [
        jnp.concatenate(
            [values[frame * spots : (frame + 1) * spots, k * wide : (k + 1) * wide] for k in range(cuts)], axis=0
        )
        for frame in range(frames)
    ]


def unpack(packed, width):
    frames, rows, wide = packed.shape
    cuts = width // wide
    spots = rows // cuts
    packed = packed.astype(F32)
    return jnp.concatenate(
        [
            jnp.concatenate([packed[frame, k * spots : (k + 1) * spots] for k in range(cuts)], axis=1)
            for frame in range(frames)
        ],
        axis=0,
    )


class Exchange:
    def __init__(self, group, stage, landing, sems):
        self.group, self.stage, self.landing, self.sems = group, stage, landing, sems

    def copy(self, block, far):
        g = self.group
        other = g.other_frame(far)
        return remote(
            self.stage.at[block, other], self.landing.at[block, g.frame], self.sems, far - 1, block, other, "frames"
        )

    def push(self, block, values):
        frames = self.group.frames
        for frame, piece in enumerate(pack(values, frames)):
            self.stage[block, frame] = piece.astype(BF)
        self.landing[block, self.group.frame] = self.stage[block, self.group.frame]
        for far in range(1, frames):
            self.copy(block, far).start()

    def arrive(self, block):
        for far in range(1, self.group.frames):
            self.copy(block, far).wait_recv()

    def sent(self, block):
        for far in range(1, self.group.frames):
            self.copy(block, far).wait_send()

    @staticmethod
    def scratch(shape):
        return [pltpu.VMEM(shape, BF), pltpu.SemaphoreType.DMA((2, shape[1] - 1, shape[0]))]


class Reduce:
    def __init__(self, group_size, slack, load, group, source, result, stage, landing, sems, own, own_sems):
        self.group_size, self.slack, self.load = group_size, slack, load
        self.group, self.source, self.result = group, source, result
        self.stage, self.landing, self.sems = stage, landing, sems
        self.own, self.own_sems = own, own_sems
        self.chunks, self.pieces = result.shape[:2]
        self.levels = group.levels

    def half(self, level):
        return self.pieces >> (level + 1)

    def choice(self, chunk, level, normal):
        turned = self.group.c * (1 - (chunk + self.chunks - 3) // self.chunks)
        return normal[level] + turned * (normal[(level + 1) % self.levels] - normal[level])

    def bit(self, chunk, level):
        return self.choice(chunk, level, self.group.bits)

    def partner(self, chunk, level):
        return self.choice(chunk, level, self.group.partners)

    def offset(self, chunk, level):
        return sum((self.bit(chunk, k) * self.half(k) for k in range(level)), 0)

    def place(self, level):
        return pl.ds(self.pieces - (self.pieces >> level), self.half(level))

    def down(self, chunk, level):
        place = self.place(level)
        return remote(
            self.stage.at[chunk, place],
            self.landing.at[chunk, place],
            self.sems,
            level,
            chunk,
            self.partner(chunk, level),
            "frames",
        )

    def up(self, chunk, level):
        done = self.result.at[chunk, pl.ds(self.offset(chunk, level + 1), self.half(level))]
        source = self.own.at[chunk] if level == self.levels - 1 else done
        return remote(source, done, self.sems, self.levels + level, chunk, self.partner(chunk, level), "frames")

    def keep(self, chunk):
        mine = self.result.at[chunk, pl.ds(self.offset(chunk, self.levels), 1)]
        return pltpu.make_async_copy(self.own.at[chunk], mine, self.own_sems.at[chunk])

    def put(self, chunk, level):
        half = self.half(level)
        given = self.offset(chunk, level) + (1 - self.bit(chunk, level)) * half
        self.stage[chunk, self.place(level)] = self.source[chunk, pl.ds(given, half)].astype(BF)
        self.down(chunk, level).start()

    def add(self, chunk, level):
        self.down(chunk, level).wait_recv()
        kept = pl.ds(self.offset(chunk, level + 1), self.half(level))
        self.source[chunk, kept] = self.source[chunk, kept] + self.landing[chunk, self.place(level)].astype(F32)

    def advance(self, chunk, turn):
        levels = self.levels
        if turn == 0:
            if self.load is not None:
                self.load.wait(chunk)
            self.put(chunk, 0)
        elif turn < levels:
            self.add(chunk, turn - 1)
            self.put(chunk, turn)
        elif turn == levels:
            self.add(chunk, levels - 1)
            mine = pl.ds(self.offset(chunk, levels), 1)
            self.own[chunk] = self.source[chunk, mine].astype(BF)
            self.keep(chunk).start()
            self.up(chunk, levels - 1).start()
        else:
            if turn == levels + 1:
                self.keep(chunk).wait()
            self.up(chunk, 2 * levels - turn).wait_recv()
            self.up(chunk, 2 * levels - turn - 1).start()

    def tick(self, time):
        for turn in range(2 * self.levels):
            first = time - turn - (self.slack if turn else 0)

            @pl.when((first >= 0) & (first < self.chunks // self.group_size))
            def _():
                for k in range(self.group_size):
                    self.advance(first * self.group_size + k, turn)

    def last(self):
        return self.chunks // self.group_size + 2 * self.levels - 2 + self.slack

    def finish(self):
        def done(chunk, carry):
            if self.levels == 1:
                self.keep(chunk).wait()
            self.up(chunk, 0).wait_recv()
            for level in range(self.levels):
                self.down(chunk, level).wait_send()
                self.up(chunk, level).wait_send()
            return carry

        lax.fori_loop(0, self.chunks, done, 0)

    @staticmethod
    def scratch(shape):
        chunks, pieces, part, width = shape
        levels = pieces.bit_length() - 1
        return [
            pltpu.VMEM((chunks, pieces - 1, part, width), BF),
            pltpu.VMEM((chunks, pieces - 1, part, width), BF),
            pltpu.SemaphoreType.DMA((2, 2 * levels, chunks)),
            pltpu.VMEM((chunks, 1, part, width), BF),
            pltpu.SemaphoreType.DMA((chunks,)),
        ]


class SmallSum:
    def __init__(self, group, total, out, landing, sems):
        self.peers = group.everyone()
        self.total, self.out, self.landing, self.sems = total, out, landing, sems

    def copy(self, turn):
        axis, peer = self.peers[turn]
        return remote(self.out.at[turn], self.landing.at[turn], self.sems, 0, turn, peer, axis)

    def tick(self, time):
        for turn in range(len(self.peers) + 1):

            @pl.when(time == turn)
            def _():
                if turn > 0:
                    self.copy(turn - 1).wait_recv()
                    self.total[...] += self.landing[turn - 1]
                if turn < len(self.peers):
                    self.out[turn] = self.total[...]
                    self.copy(turn).start()

    def last(self):
        return len(self.peers)

    def finish(self):
        for turn in range(len(self.peers)):
            self.copy(turn).wait_send()

    @staticmethod
    def scratch(peers, shape):
        return [
            pltpu.VMEM((peers,) + shape, F32),
            pltpu.VMEM((peers,) + shape, F32),
            pltpu.SemaphoreType.DMA((2, 1, peers)),
        ]


class Bulk:
    def __init__(self, group, source, landing, sems, own_sem):
        self.group, self.source, self.landing, self.sems = group, source, landing, sems
        frame = group.frame
        self.own = pltpu.make_async_copy(source.at[frame], landing.at[frame], own_sem)

    def copy(self, far):
        other = self.group.other_frame(far)
        return remote(
            self.source.at[other], self.landing.at[self.group.frame], self.sems, 0, far - 1, other, "frames"
        )

    def start(self):
        self.own.start()
        for far in range(1, self.group.frames):
            self.copy(far).start()

    def finish(self):
        self.own.wait()
        for far in range(1, self.group.frames):
            self.copy(far).wait()

    @staticmethod
    def scratch(frames):
        return [pltpu.SemaphoreType.DMA((2, 1, frames - 1)), pltpu.SemaphoreType.DMA]


class Twice:
    def __init__(self, scatter, before):
        self.scatter, self.before = scatter, before

    def cross(self, pair):
        for k in range(2):
            self.scatter.cross(2 * pair + k + self.before)


class Move:
    def __init__(self, pairs, sems, shift=0):
        self.pairs, self.sems, self.shift = pairs, sems, shift

    def copies(self, block):
        return [
            pltpu.make_async_copy(
                src.at[block % src.shape[0]], dst.at[(block + self.shift) % dst.shape[0]], self.sems.at[k, block]
            )
            for k, (src, dst) in enumerate(self.pairs)
        ]

    def start(self, block):
        for copy in self.copies(block):
            copy.start()

    def wait(self, block):
        for copy in self.copies(block):
            copy.wait()


def pipeline(phases, steps=0, beside=None):
    def step(i, carry):
        for lag in (0, 1, 2, LAG):
            first = 0
            for blocks, gathers, scatters, compute, take in phases:
                block = i - lag - first
                first += blocks

                @pl.when((block >= 0) & (block < blocks))
                def _():
                    if lag == 0:
                        for gather in gathers:
                            gather.forward(block)
                    elif lag == 1:
                        for gather in gathers:
                            gather.arrive(block)
                        compute(block)
                    elif lag == 2:
                        for scatter, before in scatters:
                            scatter.cross(block + before)
                    elif take is not None:
                        take(block)

        if beside is not None:
            beside(i)
        return carry

    lax.fori_loop(0, max(sum(phase[0] for phase in phases) + LAG, steps), step, 0)
    for scatter in {id(scatter): scatter for phase in phases for scatter, _ in phase[2]}.values():
        if isinstance(scatter, Scatter):
            scatter.finish()


def coded_rows(codes_ref, block, actions):
    return (lax.broadcasted_iota(jnp.int32, (actions, 1), 0) == codes_ref[0, block]).astype(F32)


def space_stream(stream_ref, codes_ref, table_ref, block):
    hot = coded_rows(codes_ref, block, table_ref.shape[0])
    added = jnp.sum(hot * table_ref[...].astype(F32), axis=0, keepdims=True)
    return stream_ref[block].astype(F32) + added


def row_of(gain_ref):
    return gain_ref[...].astype(F32)[None]


def attention_block(whole_ref, w_qkv_ref, w_out_ref, qkv_ref, att_ref, seen_ref):
    _, part, width = whole_ref.shape
    normed = whole_ref[...].reshape(4 * part, width)
    for member in range(3):
        qkv_ref[member] = dot(normed, w_qkv_ref[member], (1, 0)).astype(BF)
    att_ref[...] = attend(qkv_ref[0], qkv_ref[1], qkv_ref[2], seen_ref)
    return dot(att_ref[...], w_out_ref[...], (1, 0))


def each_block(blocks, work):
    def one(block, carry):
        work(block)
        return carry

    lax.fori_loop(0, blocks, one, 0)


def call(kernel, name, collective_id, operands, outs, scratch, flops):
    def specs(items):
        return [pl.BlockSpec(memory_space=space) for _, space in items]

    return pl.pallas_call(
        kernel,
        name=name,
        out_shape=[shape for shape, _ in outs],
        in_specs=specs(operands),
        out_specs=specs(outs),
        scratch_shapes=scratch,
        compiler_params=pltpu.CompilerParams(
            collective_id=collective_id, has_side_effects=True, vmem_limit_bytes=LIMIT
        ),
        cost_estimate=pl.CostEstimate(flops=flops, bytes_accessed=16 << 20, transcendentals=0),
    )(*(array for array, _ in operands))


def inside(*items):
    return [(item, pltpu.VMEM) for item in items]


def outside(*items):
    return [(item, pl.ANY) for item in items]


def scalars(item):
    return [(item, pltpu.SMEM)]


def held_like(shapes):
    return [pltpu.VMEM(shape.shape, shape.dtype) for shape in shapes] + [
        pltpu.SemaphoreType.DMA((len(shapes), shapes[0].shape[0]))
    ]


def saved_shapes(blocks, part, width, inner):
    return [
        jax.ShapeDtypeStruct((blocks, 4, part, width), BF),
        jax.ShapeDtypeStruct((blocks, 3, 4 * part, inner), BF),
        jax.ShapeDtypeStruct((blocks, 4 * part, inner), BF),
    ]


def backward_kernel(
    frames,
    grad_ref,
    stream_ref,
    tokens_ref,
    codes_ref,
    table_ref,
    gain_sp_ref,
    gain_tm_ref,
    gain_ff_out,
    w_qkv_sp_ref,
    w_out_sp_ref,
    w_qkv_tm_ref,
    w_out_tm_ref,
    *refs,
):
    time_saved, space_saved, refs = refs[:3], refs[3:6], refs[6:]
    rest_in, mixed_ref, out_ref, space_total, time_total, rest_total, small_ref, mixed_out_ref, *refs = refs
    small_clips, seen_ref, mixed_sems, own_sem, stage, stage_sems, landing, *refs = refs
    slots, refs = refs[:3], refs[3:]
    time_load_sems, space_load_sems, rest_load_sems, w_sum, shared_sum, *refs = refs
    grad_whole_ref, packed_ref, time_sems, space_sems, *refs = refs
    whole_ref, qkv_ref, att_ref = slots
    blocks, _, part, width = grad_whole_ref.shape
    rows = 4 * part
    group = Group(frames, True)
    group.meet()
    time_gather = Gather(group, grad_whole_ref, time_sems)
    space_gather = Gather(group, grad_whole_ref, space_sems)
    scatter = Scatter(group, *refs[:6])
    rest_load = Move([(rest_in, shared_sum)], rest_load_sems)
    rest_reduce = Reduce(2, 1, rest_load, group, shared_sum, rest_total, *refs[6:11])
    time_reduce = Reduce(2, 1, None, group, w_sum, time_total, *refs[11:16])
    space_reduce = Reduce(1, 0, None, group, shared_sum, space_total, *refs[6:8], *refs[16:19])
    small = SmallSum(group, small_ref, *refs[19:])
    exchange = Exchange(group, stage, landing, stage_sems)
    mixed_bulk = Bulk(group, mixed_ref, mixed_out_ref, mixed_sems, own_sem)
    time_load = Move(list(zip(time_saved, slots)), time_load_sems)
    space_load = Move(list(zip(space_saved, slots)), space_load_sems, blocks)
    ahead = whole_ref.shape[0] - 1

    def gather_grad(gather, block, grad):
        grad_whole_ref[block, group.me] = grad.astype(BF)
        gather.start(block)

    each_block(blocks, lambda block: gather_grad(time_gather, block, grad_ref[block]))
    each_block(ahead, time_load.start)
    each_block(CHUNKS, rest_load.start)
    mixed_bulk.start()
    w_sum[...] = jnp.zeros_like(w_sum)
    seen_ref[...] = visible(rows, frames, 1).astype(F32)
    small_ref[...] = jnp.zeros_like(small_ref)
    small_ref[10:11, :] = gain_ff_out[...]

    def back(block, at, w_qkv_ref):
        scatter.free(at)
        scatter.send(at, sum(dot(packed_ref[block, member], w_qkv_ref[member], (1, 1)) for member in range(3)))

    def attention(block, slot, w_out_ref, sums, seen):
        grad_y = grad_whole_ref[block].reshape(rows, width)
        grad_att = dot(grad_y, w_out_ref[...], (1, 1)).astype(BF)
        grads = attend_back(qkv_ref[slot, 0], qkv_ref[slot, 1], qkv_ref[slot, 2], grad_att, seen)
        for member in range(3):
            packed_ref[block, member] = grads[member]
        piece = sums.shape[1:]
        normed = whole_ref[slot].reshape(rows, width)
        quarter = width // 4
        for member in range(4):
            small = packed_ref[block, member] if member < 3 else att_ref[slot]
            wide = normed if member < 3 else grad_y
            grad_w = dot(small, wide, (0, 0))
            cuts = [grad_w[:, k * quarter : (k + 1) * quarter] for k in range(4)]
            for k in range(2):
                sums[2 * member + k] += jnp.concatenate(cuts[2 * k : 2 * k + 2], axis=0).reshape(piece)

    def time_compute(block):
        time_load.wait(block)

        @pl.when(block + ahead < blocks)
        def _():
            time_load.start(block + ahead)

        @pl.when(block + ahead >= blocks)
        def _():
            space_load.start(block + ahead - blocks)

        attention(block, block % (ahead + 1), w_out_tm_ref, w_sum, seen_ref)
        time_gather.sent(block)
        back(block, block, w_qkv_tm_ref)

    def time_take(block):
        stream = unpack(stream_ref[block], width)
        grad_part, grad_gain = norm_backward(scatter.take(block), stream, row_of(gain_tm_ref))
        exchange.push(block, grad_ref[block] + grad_part)
        small_ref[9:10, :] += grad_gain

    def space_compute(block):
        space_load.wait(block)

        @pl.when(block + ahead < blocks)
        def _():
            space_load.start(block + ahead)

        attention(block, (block + blocks) % (ahead + 1), w_out_sp_ref, shared_sum, None)

    def space_back(pair):
        for k in range(2):
            back(2 * pair + k, 2 * pair + k + blocks, w_qkv_sp_ref)

    def space_take(pair):
        for k in range(2):
            block = 2 * pair + k
            stream = space_stream(tokens_ref, codes_ref, table_ref, block)
            grad_part, grad_gain = norm_backward(scatter.take(block + blocks), stream, row_of(gain_sp_ref))
            grad_stream = unpack(landing[block], width) + grad_part
            out_ref[block] = grad_stream
            small_ref[8:9, :] += grad_gain
            small_clips[pl.ds(block, 1)] = jnp.sum(grad_stream, axis=0, keepdims=True)[None]

    launch_lag = LAG + 2
    space_first = blocks + GAP
    space_done = space_first + blocks
    taken = space_done + blocks // 2 + LAG - 1

    def beside(i):
        block = i - launch_lag

        @pl.when((block >= 0) & (block < blocks))
        def _():
            exchange.arrive(block)
            gather_grad(space_gather, block, unpack(landing[block], width))

        rest_reduce.tick(i)
        time_reduce.tick(i - blocks)

        @pl.when(i == space_first)
        def _():
            shared_sum[...] = jnp.zeros_like(shared_sum)

        @pl.when(i == space_done - 1)
        def _():
            rest_reduce.finish()

        space_reduce.tick(i - space_done)

        @pl.when(i == taken)
        def _():
            for clip in range(blocks):
                small_ref[0:8, :] += coded_rows(codes_ref, clip, 8) * small_clips[clip]

        small.tick(i - taken)

    pipeline(
        [
            (blocks, [time_gather], [(scatter, 0)], time_compute, time_take),
            (GAP, [], [], lambda block: None, None),
            (blocks, [space_gather], [], space_compute, None),
            (blocks // 2, [], [(Twice(scatter, blocks), 0)], space_back, space_take),
        ],
        max(space_done + space_reduce.last() + 1, taken + small.last() + 1),
        beside,
    )
    each_block(blocks, space_gather.sent)
    each_block(blocks, exchange.sent)
    for moved in (time_reduce, space_reduce, small, mixed_bulk):
        moved.finish()


def backward(frames, grad, stream, tokens, codes, table, gains, weights, kept, rest_sum, mixed):
    blocks, part, width = tokens.shape
    inner = weights[1].shape[0]
    rows = 4 * part
    packed = packed_shape(blocks, frames, part, width)
    sums = (CHUNKS, frames, 2 * inner // frames, width // 4)
    small = (16, width)
    peers = 2 + frames.bit_length() - 1
    reduce = Reduce.scratch(sums)
    return call(
        functools.partial(backward_kernel, frames),
        "backward",
        2,
        inside(grad, stream, tokens)
        + scalars(codes)
        + inside(table, *gains, *weights)
        + outside(*kept, rest_sum, mixed),
        inside(jax.ShapeDtypeStruct(tokens.shape, F32))
        + outside(*[jax.ShapeDtypeStruct(sums, BF)] * 3)
        + inside(jax.ShapeDtypeStruct(small, F32))
        + outside(jax.ShapeDtypeStruct(mixed.shape, BF)),
        [pltpu.VMEM((blocks, 1, width), F32), pltpu.VMEM((rows, rows), F32)]
        + Bulk.scratch(frames)
        + Exchange.scratch(packed)
        + [pltpu.VMEM(packed, BF)]
        + [pltpu.VMEM((3,) + each.shape[1:], BF) for each in kept[:3]]
        + [pltpu.SemaphoreType.DMA((3, blocks))] * 2
        + [pltpu.SemaphoreType.DMA((1, CHUNKS)), pltpu.VMEM(sums, F32), pltpu.VMEM(sums, F32)]
        + [pltpu.VMEM((blocks, 4, part, width), BF), pltpu.VMEM((blocks, 3, rows, inner), BF)]
        + [Gather.scratch(blocks)] * 2
        + Scatter.scratch(2 * blocks, blocks, part, width)
        + reduce
        + reduce
        + reduce[2:]
        + SmallSum.scratch(peers, small),
        1 << 30,
    )


def gelu_parts(hidden):
    slope = 0.7978845608028654
    square = hidden * hidden
    bent = jnp.tanh(slope * hidden * (1.0 + 0.044715 * square))
    half = 0.5 * (1.0 + bent)
    grad = half + 0.5 * hidden * (1.0 - bent * bent) * (slope * (1.0 + 3 * 0.044715 * square))
    return hidden * half, grad


def forward_kernel(
    frames,
    tokens_ref,
    codes_ref,
    table_ref,
    cot_in,
    gain_sp_ref,
    gain_tm_ref,
    gain_ff_ref,
    w_qkv_sp_ref,
    w_out_sp_ref,
    w_qkv_tm_ref,
    w_out_tm_ref,
    w_up_in,
    w_down_in,
    stream_ref,
    mixed_ref,
    grad_ref,
    gain_out_ref,
    total_ref,
    sum_out,
    *refs,
):
    space_saved, time_saved, refs = refs[:3], refs[3:6], refs[6:]
    w_sum, rest_sum, sum_sems, w_up_ref, w_down_ref, w_sems, *refs = refs
    whole_ref, qkv_ref, att_ref, space_sems, time_sems, seen_ref, stage, stage_sems, *refs = refs
    cot_ref, bulk_sems, own_sem, cot_whole_ref, sp_sems, tm_sems, ffn_sems, cot_sems, *refs = refs
    blocks, _, part, width = whole_ref.shape
    rows = 4 * part
    half = w_up_ref.shape[2] // 2
    group = Group(frames, True)
    group.meet()
    space_gather = Gather(group, whole_ref, sp_sems)
    time_gather = Gather(group, whole_ref, tm_sems)
    ffn_gather = Gather(group, whole_ref, ffn_sems)
    cot_gather = Gather(group, cot_whole_ref, cot_sems)
    scatter = Scatter(group, *refs[:6])
    grad_scatter = Scatter(group, *refs[6:12])
    reduce = Reduce(2, 1, None, group, w_sum, total_ref, *refs[12:])
    exchange = Exchange(group, stage, stream_ref, stage_sems)
    cot_bulk = Bulk(group, cot_in, cot_ref, bulk_sems, own_sem)
    w_load = Move([(w_up_in, w_up_ref), (w_down_in, w_down_ref)], w_sems)
    sum_save = Move([(rest_sum, sum_out)], sum_sems)

    def gather_normed(gather, block, stream, gain_ref):
        unit, _ = norm_parts(stream)
        whole_ref[block, group.me] = (unit * row_of(gain_ref)).astype(BF)
        gather.start(block)

    def begin(block):
        gather_normed(space_gather, block, space_stream(tokens_ref, codes_ref, table_ref, block), gain_sp_ref)

    each_block(blocks, begin)
    cot_bulk.start()
    w_load.start(0)
    seen_ref[...] = visible(rows, frames).astype(F32)
    w_sum[...] = jnp.zeros_like(w_sum)
    rest_sum[...] = jnp.zeros_like(rest_sum)
    gain_out_ref[...] = jnp.zeros_like(gain_out_ref)

    def attention(block, gather, saved, sems, w_qkv_ref, w_out_ref, seen, at):
        whole_save = Move([(whole_ref, saved[0])], sems.at[0:1])
        save = Move([(qkv_ref, saved[1]), (att_ref, saved[2])], sems.at[1:3])
        whole_save.start(block)

        @pl.when(block >= 2)
        def _():
            save.wait(block - 2)

        slot = block % 2
        result = attention_block(whole_ref.at[block], w_qkv_ref, w_out_ref, qkv_ref.at[slot], att_ref.at[slot], seen)
        save.start(block)
        gather.sent(block)
        whole_save.wait(block)
        scatter.free(at)
        scatter.send(at, result)

        @pl.when(block == blocks - 1)
        def _():
            save.wait(blocks - 2)
            save.wait(blocks - 1)

    def space_compute(block):
        attention(block, space_gather, space_saved, space_sems, w_qkv_sp_ref, w_out_sp_ref, None, block)

    def time_compute(block):
        at = block + blocks
        attention(block, time_gather, time_saved, time_sems, w_qkv_tm_ref, w_out_tm_ref, seen_ref, at)

    def space_take(block):
        exchange.push(block, space_stream(tokens_ref, codes_ref, table_ref, block) + scatter.take(block))

    def time_take(block):
        stream = unpack(stream_ref[block], width) + scatter.take(block + blocks)
        grad_ref[block] = stream
        gather_normed(ffn_gather, block, stream, gain_ff_ref)
        cot_whole_ref[block, group.me] = unpack(cot_ref[:, block], width).astype(BF)
        cot_gather.start(block)

    def ffn_compute(block, second):
        sums = rest_sum if second else w_sum
        hidden = pl.ds(half if second else 0, half)
        normed = whole_ref[block].reshape(rows, width)
        grad_y = cot_whole_ref[block].reshape(rows, width)
        w_up = w_up_ref[0, :, hidden]
        w_down = w_down_ref[0, hidden, :]
        activated, slope = gelu_parts(dot(normed, w_up, (1, 0)))
        activated = activated.astype(BF)
        grad_pre = (dot(grad_y, w_down, (1, 1)) * slope).astype(BF)
        if not second:
            scatter.free(block + 2 * blocks)
        for each, at, values in (
            (scatter, block + 2 * blocks, dot(activated, w_down, (1, 0))),
            (grad_scatter, block, dot(grad_pre, w_up, (1, 1))),
        ):
            if second:
                each.send(at, values, True)
            else:
                each.put(at, values)
        for first, small, wide in ((0, grad_pre, normed), (4, activated, grad_y)):
            grad_w = dot(small, wide, (0, 0))
            for k in range(4):
                cut = grad_w[:, k * (width // 4) : (k + 1) * (width // 4)]
                sums[first + k] += cut.reshape(sums.shape[1:])

    def take(block):
        stream = grad_ref[block]
        for frame, piece in enumerate(pack(stream + scatter.take(block + 2 * blocks), frames)):
            mixed_ref[frame, block] = piece.astype(BF)
        grad_part, grad_gain = norm_backward(grad_scatter.take(block), stream, row_of(gain_ff_ref))
        grad_ref[block] = cot_whole_ref[block, group.me].astype(F32) + grad_part
        gain_out_ref[...] += grad_gain

    launch_lag = LAG + 2
    ffn_first = 2 * blocks + GAP

    def beside(i):
        block = i - launch_lag

        @pl.when((block >= 0) & (block < blocks))
        def _():
            exchange.arrive(block)
            gather_normed(time_gather, block, unpack(stream_ref[block], width), gain_tm_ref)

        @pl.when(i == blocks + GAP)
        def _():
            cot_bulk.finish()

        @pl.when(i == ffn_first)
        def _():
            w_load.wait(0)

        reduce.tick(i - ffn_first - blocks)

        @pl.when(i == ffn_first + 2 * blocks)
        def _():
            each_block(CHUNKS, sum_save.start)

    pipeline(
        [
            (blocks, [space_gather], [(scatter, 0)], space_compute, space_take),
            (GAP, [], [], lambda block: None, None),
            (blocks, [time_gather], [(scatter, blocks)], time_compute, time_take),
            (blocks, [ffn_gather, cot_gather], [], lambda block: ffn_compute(block, False), None),
            (blocks, [], [(scatter, 2 * blocks), (grad_scatter, 0)], lambda block: ffn_compute(block, True), take),
        ],
        ffn_first + blocks + reduce.last() + 1,
        beside,
    )
    each_block(blocks, ffn_gather.sent)
    each_block(blocks, cot_gather.sent)
    each_block(blocks, exchange.sent)
    reduce.finish()
    each_block(CHUNKS, sum_save.wait)


def forward(frames, tokens, codes, table, cot, gains, w_qkv_sp, w_out_sp, w_qkv_tm, w_out_tm, w_up, w_down):
    blocks, part, width = tokens.shape
    inner = w_out_sp.shape[0]
    packed = packed_shape(blocks, frames, part, width)
    whole = pltpu.VMEM((blocks, 4, part, width), BF)
    saved = saved_shapes(blocks, part, width, inner)
    sums = jax.ShapeDtypeStruct((CHUNKS, frames, w_up.shape[1] // (2 * frames), width // 4), F32)
    weights = [w_up[None], w_down[None]]
    return call(
        functools.partial(forward_kernel, frames),
        "forward_and_ffn",
        1,
        inside(tokens)
        + scalars(codes)
        + inside(table)
        + outside(cot)
        + inside(*gains, w_qkv_sp, w_out_sp, w_qkv_tm, w_out_tm)
        + outside(*weights),
        inside(
            jax.ShapeDtypeStruct(packed, BF),
            jax.ShapeDtypeStruct(cot.shape, BF),
            jax.ShapeDtypeStruct((blocks, part, width), F32),
            jax.ShapeDtypeStruct((1, width), F32),
        )
        + outside(jax.ShapeDtypeStruct(sums.shape, BF), sums, *saved, *saved),
        [pltpu.VMEM(sums.shape, F32), pltpu.VMEM(sums.shape, F32), pltpu.SemaphoreType.DMA((1, CHUNKS))]
        + held_like(weights)
        + [
            whole,
            pltpu.VMEM((2,) + saved[1].shape[1:], BF),
            pltpu.VMEM((2,) + saved[2].shape[1:], BF),
            pltpu.SemaphoreType.DMA((3, blocks)),
            pltpu.SemaphoreType.DMA((3, blocks)),
            pltpu.VMEM((4 * part, 4 * part), F32),
        ]
        + Exchange.scratch(packed)
        + [pltpu.VMEM(cot.shape, BF)]
        + Bulk.scratch(frames)
        + [whole]
        + [Gather.scratch(blocks)] * 4
        + Scatter.scratch(3 * blocks, blocks, part, width)
        + Scatter.scratch(blocks, blocks, part, width)
        + Reduce.scratch(sums.shape),
        (16 * inner + 12 * w_up.shape[1]) * blocks * 4 * part * width,
    )


def widen_kernel(space_ref, time_ref, first_ref, second_ref, mixed_ref, tokens_ref, small_ref, *outs):
    step = pl.program_id(0)
    mixed_out, tokens_out, table_out, *gain_outs = outs[:6]
    for sums_ref, qkv_out, w_out_out in ((space_ref, *outs[6:8]), (time_ref, *outs[8:10])):
        quarter = sums_ref.shape[3]

        @pl.when(step < 6)
        def _():
            for k in range(2):
                qkv_out[0, k * quarter : (k + 1) * quarter] = sums_ref[0, k].T.astype(F32)

        @pl.when(step >= 6)
        def _():
            for k in range(2):
                w_out_out[:, k * quarter : (k + 1) * quarter] = sums_ref[0, k].astype(F32)

    up_out, down_out = outs[10:]
    hidden = first_ref.shape[1]

    @pl.when(step < 4)
    def _():
        for k, ffn_ref in enumerate((first_ref, second_ref)):
            up_out[:, k * hidden : (k + 1) * hidden] = ffn_ref[0].T.astype(F32)

    @pl.when(step >= 4)
    def _():
        for k, ffn_ref in enumerate((first_ref, second_ref)):
            down_out[k * hidden : (k + 1) * hidden] = ffn_ref[0].astype(F32)

    for block in range(mixed_ref.shape[1]):
        mixed_out[block] = unpack(mixed_ref[:, block], mixed_out.shape[2]).astype(BF)
    tokens_out[...] = tokens_ref[...]

    @pl.when(step == 0)
    def _():
        table_out[...] = small_ref[0:8, :]
        for k, gain_out in enumerate(gain_outs):
            gain_out[...] = small_ref[8 + k : 9 + k, :]


def widen(frames, space_sums, time_sums, first_sums, second_sums, mixed, tokens, small, inner):
    blocks, part, width = tokens.shape
    quarter = width // 4
    hidden = 2 * first_sums.shape[1] * first_sums.shape[2]
    whole = lambda i: (0, 0)
    some = pl.BlockSpec((blocks // CHUNKS, part, width), lambda i: (i, 0, 0))
    turned = [
        (
            jax.ShapeDtypeStruct((3, width, inner), F32),
            pl.BlockSpec((1, 2 * quarter, inner), lambda i: (jnp.minimum(i, 5) // 2, jnp.minimum(i, 5) % 2, 0)),
        ),
        (
            jax.ShapeDtypeStruct((inner, width), F32),
            pl.BlockSpec((inner, 2 * quarter), lambda i: (0, jnp.maximum(i - 6, 0))),
        ),
    ]
    outs = [(jax.ShapeDtypeStruct(tokens.shape, BF), some), (jax.ShapeDtypeStruct(tokens.shape, F32), some)]
    outs += [(jax.ShapeDtypeStruct((8, width), F32), pl.BlockSpec((8, width), whole))]
    outs += [(jax.ShapeDtypeStruct((1, width), F32), pl.BlockSpec((1, width), whole))] * 3 + turned + turned
    outs += [
        (
            jax.ShapeDtypeStruct((width, hidden), F32),
            pl.BlockSpec((quarter, hidden), lambda i: (jnp.minimum(i, 3), 0)),
        ),
        (
            jax.ShapeDtypeStruct((hidden, width), F32),
            pl.BlockSpec((hidden, quarter), lambda i: (0, jnp.maximum(i - 4, 0))),
        ),
    ]
    chunk = pl.BlockSpec((1, 2, inner, quarter), lambda i: (i, 0, 0, 0))
    ffn_chunk = pl.BlockSpec((1, hidden // 2, quarter), lambda i: (i, 0, 0))
    return pl.pallas_call(
        widen_kernel,
        name="widen",
        grid=(CHUNKS,),
        out_shape=[shape for shape, _ in outs],
        in_specs=[
            chunk,
            chunk,
            ffn_chunk,
            ffn_chunk,
            pl.BlockSpec((frames, blocks // CHUNKS) + mixed.shape[2:], lambda i: (0, i, 0, 0)),
            some,
            pl.BlockSpec(small.shape, whole),
        ],
        out_specs=[spec for _, spec in outs],
        compiler_params=pltpu.CompilerParams(vmem_limit_bytes=LIMIT),
    )(
        space_sums.reshape(CHUNKS, 2, inner, quarter),
        time_sums.reshape(CHUNKS, 2, inner, quarter),
        first_sums.reshape(CHUNKS, hidden // 2, quarter),
        second_sums.reshape(CHUNKS, hidden // 2, quarter),
        mixed,
        tokens,
        small,
    )


def pack_rows(values, frames):
    blocks, part, width = values.shape
    shape = packed_shape(blocks, frames, part, width)
    cut = values.reshape(blocks, frames, part // frames, width // shape[-1], shape[-1])
    return cut.transpose(1, 0, 3, 2, 4).reshape((frames, blocks) + shape[2:])


def body(
    frames,
    tokens,
    codes,
    table,
    gain_space,
    gain_time,
    gain_ffn,
    w_qkv_space,
    w_out_space,
    w_qkv_time,
    w_out_time,
    w_up,
    w_down,
    cotangent,
):
    gain_sp, gain_tm, gain_ff = gain_space, gain_time, gain_ffn
    w_qkv_sp = w_qkv_space.swapaxes(0, 1)
    w_qkv_tm = w_qkv_time.swapaxes(0, 1)
    _, blocks, part, width = tokens.shape

    gains = gain_sp, gain_tm, gain_ff
    weights = w_qkv_sp, w_out_space, w_qkv_tm, w_out_time, w_up, w_down
    stream_one, mixed, grad_two, grad_gain_ff, first_totals, ffn_sums, *kept = forward(
        frames, tokens[0], codes, table, pack_rows(cotangent[0], frames), gains, *weights
    )
    grad_zero, space_totals, time_totals, ffn_totals, small, mixed = backward(
        frames,
        grad_two,
        stream_one,
        tokens[0],
        codes,
        table,
        (gain_sp, gain_tm, grad_gain_ff),
        weights[:4],
        kept[3:] + kept[:3],
        ffn_sums,
        mixed,
    )
    mixed, grad_zero, grad_tab, gain_sp, gain_tm, gain_ff, *grads = widen(
        frames, space_totals, time_totals, first_totals, ffn_totals, mixed, grad_zero, small, w_out_space.shape[0]
    )
    return (
        mixed[None],
        grad_zero[None],
        grad_tab,
        gain_sp[0],
        gain_tm[0],
        gain_ff[0],
        grads[0].swapaxes(0, 1),
        grads[1],
        grads[2].swapaxes(0, 1),
        grads[3],
        *grads[4:],
    )


def solution(mesh):
    rows = P("frames", None, "tensor", None)
    return jax.shard_map(
        functools.partial(body, mesh.shape["frames"]),
        mesh=mesh,
        in_specs=(
            rows,
            P("frames", None),
            P(),
            P(),
            P(),
            P(),
            P(None, None, "tensor"),
            P("tensor", None),
            P(None, None, "tensor"),
            P("tensor", None),
            P(None, "tensor"),
            P("tensor", None),
            rows,
        ),
        out_specs=(
            rows,
            rows,
            P(),
            P(),
            P(),
            P(),
            P(None, None, "tensor"),
            P("tensor", None),
            P(None, None, "tensor"),
            P("tensor", None),
            P(None, "tensor"),
            P("tensor", None),
        ),
        check_vma=False,
    )
```
